256 devices in a mesh: dp: 4 (over y), ctx: 64 (over x, z, core).
Axes of the slice: x: 4, y: 4, z: 8, core: 2. Of those that a mesh axis runs over, the one named last changes fastest.
Arguments:
- incoming_embeddings: float32 [4, 65536, 384], P('dp', 'ctx'), may hold values from -58 to 58
- stacked_projector: float32 [384, 1152], replicated, may hold values from -0.3125 to 0.3125
- final_projector: float32 [384, 384], replicated, may hold values from -0.3125 to 0.3125
- sharpness_per_view: float32 [8], replicated, may hold values from 0.5 to 3
- upstream_sensitivity: float32 [4, 65536, 384], P('dp', 'ctx'), may hold values from -6 to 6
Outputs:
- input_grad: float32 [4, 65536, 384], P('dp', 'ctx')
- mixer_grad: float32 [384, 1152], P('ctx')
- output_grad: float32 [384, 384], P('ctx')
- sharpness_sensitivity: float32 [8], replicated
The draws below stay inside these ranges and needn't reach their ends.
All inputs are finite; a program needn't handle non-finite values.
Results may differ from the reference program's by a relative error of at most 0.000088.
Values sent between devices are 32-bit elements; how exact they have to be, the bound alone decides.
No kernel may reach another device: no remote copies, remote signals or barrier semaphores. Data moves between devices by JAX's collectives and lax.ppermute only.
A program may use at most 64 MiB of HBM per device.

```python
import math
import jax
import jax.numpy as jnp
from jax import lax

PARALLEL_VIEWS = 8
D = 384
TOKENS = 65536
SLIDES = 4


def draw_incoming_embeddings(key, part):
    key = jax.random.fold_in(key, 11)
    jitter_key, column_key, base_key = jax.random.split(key, 3)
    position = jnp.arange(TOKENS, dtype=jnp.float32) / TOKENS
    jitter = jax.random.uniform(jitter_key, (SLIDES, TOKENS), jnp.float32)
    spread = math.log(10.0)
    base = jax.random.normal(base_key, (SLIDES, TOKENS, D), jnp.float32)
    base = jnp.clip(base, -4.0, 4.0)
    row_scale = jnp.exp(spread * 0.5 * (position[None, :] + jitter))
    column_scale = jnp.exp(spread * jax.random.uniform(column_key, (D,), jnp.float32))
    return (base * row_scale[:, :, None] * column_scale / 10.0).astype(jnp.float32)


def levels(own_key, extent, cuts, least, largest):
    def one(dim, parts):
        heights = jax.random.uniform(jax.random.fold_in(jax.random.fold_in(own_key, 6), dim), (parts,), jnp.float32, least / len(cuts), largest / len(cuts))
        return jnp.repeat(jnp.exp(heights), extent[dim] // parts).reshape((-1,) + (1,) * (len(extent) - dim - 1))

    loudness = one(*cuts[0])
    for cut in cuts[1:]:
        loudness = loudness * one(*cut)
    return loudness


def centred(own_key, extent, deviation, bound, shards=(), kind=jnp.bfloat16):
    factor_of = levels(own_key, extent, shards, -0.22, 0.18) if shards else 1.0
    drawn = jax.random.normal(own_key, extent, jnp.float32) * deviation * factor_of
    return jnp.minimum(jnp.maximum(drawn, -bound), bound).astype(kind)


def setup_inputs(seed: int = 0) -> dict:
    splits = jax.random.split(jax.random.key(seed), 6)
    incoming_embeddings = draw_incoming_embeddings(jax.random.fold_in(splits[5], 71), 0)
    stacked_projector = centred(splits[1], (D, 3 * D), D ** -0.5, 0.3125, (), jnp.float32)
    final_projector = centred(splits[2], (D, D), D ** -0.5, 0.3125, (), jnp.float32)
    sharpness_per_view = jnp.clip(jnp.exp(jax.random.uniform(splits[3], (PARALLEL_VIEWS,), jnp.float32, math.log(0.5), math.log(3.0))), 0.5, 3.0)
    upstream_sensitivity = centred(splits[4], (SLIDES, TOKENS, D), 1.0, 6.0, ((0, 4), (1, 64)), jnp.float32)
    return dict(incoming_embeddings=incoming_embeddings, stacked_projector=stacked_projector, final_projector=final_projector, sharpness_per_view=sharpness_per_view, upstream_sensitivity=upstream_sensitivity)


precise = lax.Precision.HIGHEST
epsilon = 1e-06

def specimen_blend_apply(patch_lines, stacked_projector, final_projector, sharpness_per_view):
    features = patch_lines.shape[1]
    view_total = sharpness_per_view.shape[0]
    projected = jnp.dot(patch_lines, stacked_projector, precision=precise)
    queries = projected[:, :features]
    keys_part = projected[:, features:2 * features]
    values_part = projected[:, 2 * features:]
    query_norm = jnp.sqrt(lax.optimization_barrier(jnp.sum(queries * queries, axis=0)) + epsilon)
    key_norm = jnp.sqrt(lax.optimization_barrier(jnp.sum(keys_part * keys_part, axis=0)) + epsilon)
    query_hat = (queries / query_norm).reshape(patch_lines.shape[0], view_total, -1)
    key_hat = (keys_part / key_norm).reshape(patch_lines.shape[0], view_total, -1)
    feature_crosscorr = jnp.einsum('nhi,nhj->hij', query_hat, key_hat, precision=precise)
    logit_table = jnp.exp(sharpness_per_view[:, None, None] * feature_crosscorr)
    attention = logit_table / lax.optimization_barrier(jnp.sum(logit_table, axis=-1, keepdims=True))
    mixed = jnp.einsum('hij,nhj->nhi', attention, values_part.reshape(patch_lines.shape[0], view_total, -1), precision=precise)
    return jnp.dot(mixed.reshape(patch_lines.shape[0], features), final_projector, precision=precise)

def reference(incoming_embeddings, stacked_projector, final_projector, sharpness_per_view, upstream_sensitivity):

    def one_slide(pair):
        patch_lines, incoming = pair
        blended_result, reverse_rule = jax.vjp(specimen_blend_apply, patch_lines, stacked_projector, final_projector, sharpness_per_view)
        return reverse_rule(incoming)
    input_grad, mixer_terms, output_terms, temp_terms = lax.map(one_slide, (incoming_embeddings, upstream_sensitivity))
    logit_multiplier = 1.0 / math.sqrt(SLIDES * TOKENS)
    return (input_grad, lax.optimization_barrier(jnp.sum(mixer_terms, axis=0)) * logit_multiplier, lax.optimization_barrier(jnp.sum(output_terms, axis=0)) * logit_multiplier, lax.optimization_barrier(jnp.sum(temp_terms, axis=0)) * logit_multiplier)
```

```python
import functools
import math

import jax
import jax.numpy as jnp
from jax import lax
from jax.experimental import pallas as pl
from jax.experimental.pallas import tpu as pltpu
from jax.sharding import Mesh, PartitionSpec as P

epsilon = 1e-06
D = 384
VIEWS = 8
HEAD = D // VIEWS
T = 128
X_CHIPS, Z_CHIPS, CORES = 4, 8, 2
SHARES = X_CHIPS * Z_CHIPS
ROWS = D // (SHARES * CORES)
A_BLOCKS = [(0, 0), (0, 1), (0, 2), (1, 1), (1, 2), (2, 2)]
B_BLOCKS = [(i, j) for i in range(3) for j in range(3)]
HALF = 8 * T
f32, bf16 = jnp.float32, jnp.bfloat16


def split(a):
    high = a.astype(bf16)
    return high, (a - high.astype(f32)).astype(bf16)


def dot3(a, b, dims):
    d = functools.partial(
        lax.dot_general, dimension_numbers=(dims, ((), ())), preferred_element_type=f32
    )
    return d(a[0], b[0]) + (d(a[0], b[1]) + d(a[1], b[0]))


NN = ((1,), (0,))
NT = ((1,), (1,))
TN = ((0,), (0,))


def gram_kernel(core_ref, x_ref, u_ref, keep_ref, send_ref, acc_ref, pay_ref):
    step = pl.program_id(0)
    xh, xl = split(x_ref[...])
    uh, ul = split(u_ref[...])
    d = functools.partial(
        lax.dot_general, dimension_numbers=(TN, ((), ())), preferred_element_type=f32
    )
    whole = d(xh, xh)
    cross = d(xh, xl)
    mixed = d(xh, uh) + (d(xh, ul) + d(xl, uh))

    @pl.when(step == 0)
    def _():
        acc_ref[0] = whole
        acc_ref[1] = cross
        acc_ref[2] = mixed

    @pl.when(step > 0)
    def _():
        acc_ref[0] += whole
        acc_ref[1] += cross
        acc_ref[2] += mixed

    @pl.when(step == pl.num_programs(0) - 1)
    def _():
        a = acc_ref[0] + acc_ref[1] + acc_ref[1].T
        at = 0
        for i, j in A_BLOCKS:
            pay_ref[at // 8, at % 8] = a[i * T : (i + 1) * T, j * T : (j + 1) * T]
            at += 1
        for i, j in B_BLOCKS:
            pay_ref[at // 8, at % 8] = acc_ref[2, i * T : (i + 1) * T, j * T : (j + 1) * T]
            at += 1
        pay_ref[1, 7] = jnp.zeros((T, T), f32)
        core = core_ref[0]
        keep_ref[...] = pay_ref[core].reshape(HALF, T)
        send_ref[...] = pay_ref[1 - core].reshape(HALF, T)


def solve_kernel(
    place_ref,
    sharp_ref,
    mine_ref,
    other_ref,
    w_ref,
    f_ref,
    ph_ref,
    pl_ref,
    rows_ref,
    a_ref,
    b_ref,
):
    core = place_ref[0]
    first = place_ref[1]
    mine = mine_ref[...].reshape(8, T, T)
    other = other_ref[...].reshape(8, T, T)
    low = jnp.where(core == 0, mine, other)
    high = jnp.where(core == 0, other, mine)
    at = 0
    for i, j in A_BLOCKS:
        block = low[at]
        a_ref[i * T : (i + 1) * T, j * T : (j + 1) * T] = block
        if i != j:
            a_ref[j * T : (j + 1) * T, i * T : (i + 1) * T] = block.T
        at += 1
    for i, j in B_BLOCKS:
        block = low[at] if at < 8 else high[at - 8]
        b_ref[i * T : (i + 1) * T, j * T : (j + 1) * T] = block
        at += 1

    wq, wk, wv = w_ref[:, :D], w_ref[:, D : 2 * D], w_ref[:, 2 * D :]
    wqs, wks, wvs, fs = split(wq), split(wk), split(wv), split(f_ref[...])
    a_s = split(a_ref[...])
    b_s = split(b_ref[...])

    row = lax.broadcasted_iota(jnp.int32, (D, D), 0)
    col = lax.broadcasted_iota(jnp.int32, (D, D), 1)
    eye = row == col
    same = jnp.zeros((D, D), jnp.bool_)
    sharp = jnp.zeros((D, 1), f32)
    for h in range(VIEWS):
        lo, hi = h * HEAD, (h + 1) * HEAD
        same = same | ((row >= lo) & (row < hi) & (col >= lo) & (col < hi))
        r = row[:, :1]
        sharp = jnp.where((r >= lo) & (r < hi), sharp_ref[h], sharp)

    def to_col(v):
        return jnp.sum(jnp.where(eye, v, 0.0), axis=1, keepdims=True)

    def to_row(v):
        return jnp.sum(jnp.where(eye, v, 0.0), axis=0, keepdims=True)

    tq = dot3(a_s, wqs, NN)
    tk = dot3(a_s, wks, NN)
    q_square = jnp.maximum(jnp.sum(wq * tq, axis=0, keepdims=True), 0.0) + epsilon
    k_square = jnp.maximum(jnp.sum(wk * tk, axis=0, keepdims=True), 0.0) + epsilon
    q_inv = lax.rsqrt(q_square)
    k_inv = lax.rsqrt(k_square)
    q_inv_col = to_col(q_inv)
    cov = dot3(wqs, split(tk), TN) * q_inv_col * k_inv
    c = dot3(wvs, b_s, TN)
    c_s = split(c)
    attention_grad = dot3(fs, c_s, NT)

    table = jnp.where(same, jnp.exp(jnp.where(same, sharp * cov, 0.0)), 0.0)
    attention = table / jnp.sum(table, axis=1, keepdims=True)
    inner = jnp.sum(attention * attention_grad, axis=1, keepdims=True)
    score_grad = attention * (attention_grad - inner)
    weighed = score_grad * cov
    cov_grad = sharp * score_grad
    inner_grad = sharp * weighed
    c_q = to_row(jnp.sum(inner_grad, axis=1, keepdims=True))
    c_k = jnp.sum(inner_grad, axis=0, keepdims=True)
    m_s = split(cov_grad * q_inv_col * k_inv)
    att_s = split(attention)

    gq = dot3(wks, m_s, NT) - wq * (c_q * q_inv * q_inv)
    gk = dot3(wqs, m_s, NN) - wk * (c_k * k_inv * k_inv)
    gv = dot3(fs, att_s, TN)
    gq_s, gk_s, gv_s = split(gq), split(gk), split(gv)
    p = dot3(gq_s, wqs, NT) + dot3(gk_s, wks, NT)
    r = dot3(gv_s, wvs, NT)
    ph, plo = split(p)
    rh, rlo = split(r)
    ph_ref[:D] = ph
    ph_ref[D:] = rh
    pl_ref[:D] = plo
    pl_ref[D:] = rlo

    pick_row = lax.broadcasted_iota(jnp.int32, (16, D), 0)
    pick_col = lax.broadcasted_iota(jnp.int32, (16, D), 1)
    pick = jnp.where(pick_row + first == pick_col, 1.0, 0.0).astype(bf16)

    def rows_of(pair):
        return tuple(jnp.dot(pick, one, preferred_element_type=f32).astype(bf16) for one in pair)

    a_rows, b_rows, att_rows = rows_of(a_s), rows_of(b_s), rows_of(att_s)
    scale = place_scale
    rows_ref[:, :D] = dot3(a_rows, gq_s, NN)[:8] * scale
    rows_ref[:, D : 2 * D] = dot3(a_rows, gk_s, NN)[:8] * scale
    rows_ref[:, 2 * D : 3 * D] = dot3(b_rows, gv_s, NN)[:8] * scale
    rows_ref[:, 3 * D : 4 * D] = dot3(att_rows, c_s, NN)[:8] * scale
    by_feature = jnp.sum(weighed, axis=1, keepdims=True) * scale
    lane = lax.broadcasted_iota(jnp.int32, (D, T), 1)
    feature = lax.broadcasted_iota(jnp.int32, (D, T), 0)
    chosen = (feature >= lane * HEAD) & (feature < (lane + 1) * HEAD)
    temp = jnp.sum(jnp.where(chosen, by_feature, 0.0), axis=0, keepdims=True)
    rows_ref[:, 4 * D :] = jnp.broadcast_to(temp, (8, T))


place_scale = 1.0 / math.sqrt(262144)


def output_kernel(x_ref, u_ref, ph_ref, pl_ref, out_ref):
    xh, xl = split(x_ref[...])
    uh, ul = split(u_ref[...])
    high = jnp.concatenate([xh, uh], axis=1)
    low = jnp.concatenate([xl, ul], axis=1)
    out_ref[...] = dot3((high, low), (ph_ref[...], pl_ref[...]), NN)


def body(
    incoming_embeddings,
    stacked_projector,
    final_projector,
    sharpness_per_view,
    upstream_sensitivity,
):
    x = incoming_embeddings[0]
    u = upstream_sensitivity[0]
    tokens = x.shape[0]
    core = lax.axis_index("core")
    ctx = (lax.axis_index("x") * Z_CHIPS + lax.axis_index("z")) * CORES + core
    place = jnp.stack([core, ctx * ROWS]).astype(jnp.int32)
    smem = pl.BlockSpec(memory_space=pltpu.SMEM)
    params = pltpu.CompilerParams(vmem_limit_bytes=48 * 1024 * 1024)

    block = tokens // 2
    token_spec = pl.BlockSpec((block, D), lambda i: (i, 0))
    half_spec = pl.BlockSpec((HALF, T), lambda i: (0, 0))
    half_shape = jax.ShapeDtypeStruct((HALF, T), f32)
    keep, send = pl.pallas_call(
        gram_kernel,
        grid=(tokens // block,),
        in_specs=[smem, token_spec, token_spec],
        out_specs=[half_spec, half_spec],
        out_shape=[half_shape, half_shape],
        scratch_shapes=[pltpu.VMEM((3, D, D), f32), pltpu.VMEM((2, 8, T, T), f32)],
        compiler_params=params,
    )(place, x, u)

    swap = [(0, 1), (1, 0)]
    part = (keep + lax.ppermute(send, "core", swap)).reshape(SHARES, -1, T)
    arrived = lax.all_to_all(part, ("x", "z"), 0, 0, tiled=True)
    summed = jnp.sum(arrived, axis=0)
    spread = jnp.broadcast_to(summed, (SHARES,) + summed.shape)
    mine = lax.all_to_all(spread, ("x", "z"), 0, 0, tiled=True).reshape(HALF, T)
    other = lax.ppermute(mine, "core", swap)

    vmem = pl.BlockSpec(memory_space=pltpu.VMEM)
    ph, plo, rows = pl.pallas_call(
        solve_kernel,
        in_specs=[smem, smem, vmem, vmem, vmem, vmem],
        out_specs=[vmem, vmem, vmem],
        out_shape=[
            jax.ShapeDtypeStruct((2 * D, D), bf16),
            jax.ShapeDtypeStruct((2 * D, D), bf16),
            jax.ShapeDtypeStruct((8, 4 * D + T), f32),
        ],
        scratch_shapes=[
            pltpu.VMEM((D, D), f32),
            pltpu.VMEM((D, D), f32),
        ],
        compiler_params=params,
    )(place, sharpness_per_view, mine, other, stacked_projector, final_projector)

    slides = lax.axis_size("dp")
    others = [
        lax.ppermute(rows, "dp", [(i, (i + k) % slides) for i in range(slides)])
        for k in range(1, slides)
    ]

    whole_spec = pl.BlockSpec((2 * D, D), lambda i: (0, 0))
    input_grad = pl.pallas_call(
        output_kernel,
        grid=(tokens // block,),
        in_specs=[token_spec, token_spec, whole_spec, whole_spec],
        out_specs=token_spec,
        out_shape=jax.ShapeDtypeStruct((tokens, D), f32),
        compiler_params=params,
        cost_estimate=pl.CostEstimate(
            flops=2 * 3 * tokens * 2 * D * D, bytes_accessed=3 * tokens * D * 4, transcendentals=0
        ),
    )(x, u, ph, plo)

    total = (rows + others[1]) + (others[0] + others[2])
    return (
        input_grad[None],
        total[:ROWS, : 3 * D],
        total[:ROWS, 3 * D : 4 * D],
        total[0, 4 * D : 4 * D + VIEWS],
    )


def solution(mesh):
    slides = mesh.shape["dp"]
    fine = Mesh(
        mesh.devices.reshape(slides, X_CHIPS, Z_CHIPS, CORES), ("dp", "x", "z", "core")
    )
    ctx = ("x", "z", "core")
    return jax.shard_map(
        body,
        mesh=fine,
        in_specs=(P("dp", ctx, None), P(), P(), P(), P("dp", ctx, None)),
        out_specs=(P("dp", ctx, None), P(ctx, None), P(ctx, None), P()),
        check_vma=False,
    )
```

```python
import functools
import math

import jax
import jax.numpy as jnp
from jax import lax
from jax.experimental import pallas as pl
from jax.experimental.pallas import tpu as pltpu
from jax.sharding import Mesh, PartitionSpec as P

epsilon = 1e-06
D = 384
VIEWS = 8
HEAD = D // VIEWS
T = 128
W = 256
X_CHIPS, Z_CHIPS, CORES = 4, 8, 2
SHARES = X_CHIPS * Z_CHIPS
ROWS = D // (SHARES * CORES)
HALF = 8 * T
QUARTER = HALF // X_CHIPS
PICK = 16
BLOCKS = [("a", i, j) for i in range(3) for j in range(i, 3)]
BLOCKS += [("b", i, j) for i in range(3) for j in range(3)]


def place_of(at):
    return at // 8, at % 8 // 2, at % 2


f32, bf16 = jnp.float32, jnp.bfloat16
NN = ((1,), (0,))
NT = ((1,), (1,))
TN = ((0,), (0,))


def split(a):
    high = a.astype(bf16)
    return high, (a - high.astype(f32)).astype(bf16)


def dot3(a, b, dims):
    d = functools.partial(
        lax.dot_general, dimension_numbers=(dims, ((), ())), preferred_element_type=f32
    )
    return d(a[0], b[0]) + (d(a[0], b[1]) + d(a[1], b[0]))


def cut(pair, rows, cols):
    return pair[0][rows, cols], pair[1][rows, cols]


ALL = slice(None)
WINDOWS = (slice(0, W), slice(D - W, D))


def join(parts):
    one, two = parts
    return jnp.concatenate([one[:, :T], one[:, T:] + two[:, :T], two[:, T:]], axis=1)


def gram_kernel(place_ref, x_hbm, u_hbm, keep_ref, send_ref, x_ref, u_ref, pay_ref, sems):
    tokens = x_ref.shape[0]
    step = tokens // 4
    copies = []
    for at, (source, target) in enumerate(((x_hbm, x_ref), (u_hbm, u_ref))):
        for k in range(4):
            piece = pl.ds(k * step, step)
            copy = pltpu.make_async_copy(source.at[piece], target.at[piece], sems.at[at * 4 + k])
            copy.start()
            copies.append(copy)
    for copy in copies[:4]:
        copy.wait()
    d = functools.partial(
        lax.dot_general, dimension_numbers=(TN, ((), ())), preferred_element_type=f32
    )
    xh, xl = split(x_ref[...])
    cross = d(xh, xl)
    grams = {"a": d(xh, xh) + cross + cross.T}
    for copy in copies[4:]:
        copy.wait()
    uh, ul = split(u_ref[...])
    grams["b"] = d(xh, uh) + (d(xh, ul) + d(xl, uh))
    for at, (name, i, j) in enumerate(BLOCKS):
        pay_ref[place_of(at)] = grams[name][i * T : (i + 1) * T, j * T : (j + 1) * T]
    pay_ref[place_of(15)] = jnp.zeros((T, T), f32)
    core, chip = place_ref[0], place_ref[2]
    for k in range(X_CHIPS):
        to = lax.rem(chip + k, X_CHIPS)
        piece = pl.ds(k * QUARTER, QUARTER)
        keep_ref[piece] = pay_ref[core, to].reshape(QUARTER, T)
        send_ref[piece] = pay_ref[1 - core, to].reshape(QUARTER, T)


def heads_of(shape, axis, window):
    feature = lax.broadcasted_iota(jnp.int32, shape, axis) + window * (D - W)
    head = jnp.zeros(shape, jnp.int32)
    for h in range(1, VIEWS):
        head = head + jnp.where(feature >= h * HEAD, 1, 0)
    return feature, head


def masks(window):
    _, rows = heads_of((W, W), 0, window)
    _, cols = heads_of((W, W), 1, window)
    own = (rows < VIEWS // 2) if window == 0 else (rows >= VIEWS // 2)
    return (rows == cols) & own


def eye_of(size):
    return lax.broadcasted_iota(jnp.int32, (size, size), 0) == lax.broadcasted_iota(
        jnp.int32, (size, size), 1
    )


def to_col(eye, v):
    return jnp.sum(jnp.where(eye, v, 0.0), axis=1, keepdims=True)


def to_row(eye, v):
    return jnp.sum(jnp.where(eye, v, 0.0), axis=0, keepdims=True)


def sharp_col(sharp_ref, window):
    _, head = heads_of((W, 1), 0, window)
    sharp = jnp.zeros((W, 1), f32)
    for h in range(VIEWS):
        sharp = jnp.where(head == h, sharp_ref[h], sharp)
    return sharp


def pick_of(first, size, offset):
    row = lax.broadcasted_iota(jnp.int32, (PICK, size), 0) + first
    col = lax.broadcasted_iota(jnp.int32, (PICK, size), 1) + offset
    return jnp.where(row == col, 1.0, 0.0).astype(bf16)


def rows_of(pick, pair):
    return tuple(jnp.dot(pick, one, preferred_element_type=f32).astype(bf16) for one in pair)


scale = 1.0 / math.sqrt(262144)


def solve_kernel(
    place_ref, sharp_ref, mine_ref, other_ref, w_ref, f_ref,
    att_ref, m_ref, d_ref, rows_ref, block_ref, a_ref, b_ref,
):
    core, first, chip = place_ref[0], place_ref[1], place_ref[2]
    for k in range(X_CHIPS):
        origin = lax.rem(chip + X_CHIPS - k, X_CHIPS)
        piece = pl.ds(k * QUARTER, QUARTER)
        block_ref[core, origin] = mine_ref[piece].reshape(2, T, T)
        block_ref[1 - core, origin] = other_ref[piece].reshape(2, T, T)
    for at, (name, i, j) in enumerate(BLOCKS):
        block = block_ref[place_of(at)]
        ref = a_ref if name == "a" else b_ref
        ref[i * T : (i + 1) * T, j * T : (j + 1) * T] = block
        if name == "a" and i != j:
            ref[j * T : (j + 1) * T, i * T : (i + 1) * T] = block.T
    a_s, b_s = split(a_ref[...]), split(b_ref[...])
    wq, wk = w_ref[:, :D], w_ref[:, D : 2 * D]
    wqs, wks, wvs, fs = split(wq), split(wk), split(w_ref[:, 2 * D :]), split(f_ref[...])
    tq = dot3(a_s, wqs, NN)
    tk = dot3(a_s, wks, NN)
    c_s = split(dot3(wvs, b_s, TN))
    q_inv = lax.rsqrt(jnp.maximum(jnp.sum(wq * tq, axis=0, keepdims=True), 0.0) + epsilon)
    k_inv = lax.rsqrt(jnp.maximum(jnp.sum(wk * tk, axis=0, keepdims=True), 0.0) + epsilon)
    tks = split(tk)
    pick = pick_of(first, D, 0)
    tq_rows, tk_rows = rows_of(pick, split(tq)), rows_of(pick, tks)
    b_f = split(dot3(rows_of(pick, b_s), fs, NT))
    eye = eye_of(W)
    q_sum, k_sum, q_rows, k_rows, v_rows, att_high, att_low = [], [], [], [], [], [], []
    temp = jnp.zeros((1, T), f32)
    for window, span in enumerate(WINDOWS):
        same = masks(window)
        sharp = sharp_col(sharp_ref, window)
        q_col = to_col(eye, q_inv[:, span])
        cov = dot3(cut(wqs, ALL, span), cut(tks, ALL, span), TN)
        cov = jnp.where(same, cov * q_col * k_inv[:, span], 0.0)
        table = jnp.where(same, jnp.exp(sharp * cov), 0.0)
        total = jnp.sum(table, axis=1, keepdims=True)
        attention = table / jnp.where(total > 0.0, total, 1.0)
        attention_grad = dot3(cut(fs, span, ALL), cut(c_s, span, ALL), NT)
        inner = jnp.sum(attention * attention_grad, axis=1, keepdims=True)
        score_grad = attention * (attention_grad - inner)
        weighed = score_grad * cov
        by_feature = jnp.sum(weighed, axis=1, keepdims=True)
        q_sum.append(to_row(eye, sharp * by_feature))
        k_sum.append(jnp.sum(sharp * weighed, axis=0, keepdims=True))
        m_s = split(sharp * score_grad * q_col * k_inv[:, span])
        m_ref[0, window], m_ref[1, window] = m_s
        att_s = split(attention)
        att_ref[0, window], att_ref[1, window] = att_s
        q_rows.append(dot3(cut(tk_rows, ALL, span), m_s, NT))
        k_rows.append(dot3(cut(tq_rows, ALL, span), m_s, NN))
        v_rows.append(dot3(cut(b_f, ALL, span), att_s, NN))
        high, low = rows_of(pick_of(first, W, window * (D - W)), att_s)
        att_high.append(high)
        att_low.append(low)
        _, head = heads_of((W, T), 0, window)
        lane = lax.broadcasted_iota(jnp.int32, (W, T), 1)
        temp += jnp.sum(jnp.where(head == lane, by_feature, 0.0), axis=0, keepdims=True)
    d_q = join(q_sum) * (q_inv * q_inv)
    d_k = join(k_sum) * (k_inv * k_inv)
    d_ref[0:1] = d_q
    d_ref[1:2] = d_k
    both = [high.astype(f32) + low.astype(f32) for high, low in (tq_rows, tk_rows)]
    rows_ref[:, :D] = (join(q_rows) - both[0] * d_q)[:8] * scale
    rows_ref[:, D : 2 * D] = (join(k_rows) - both[1] * d_k)[:8] * scale
    rows_ref[:, 2 * D : 3 * D] = join(v_rows)[:8] * scale
    rows_ref[:, 3 * D : 4 * D] = dot3((join(att_high), join(att_low)), c_s, NN)[:8] * scale
    rows_ref[:, 4 * D :] = jnp.broadcast_to(temp * scale, (8, T))


def output_kernel(x_ref, u_ref, w_ref, f_ref, att_ref, m_ref, d_ref, out_hbm, out_ref, sems):
    wq, wk = w_ref[:, :D], w_ref[:, D : 2 * D]
    wqs, wks, wvs, fs = split(wq), split(wk), split(w_ref[:, 2 * D :]), split(f_ref[...])
    q_parts, k_parts, v_parts = [], [], []
    for window, span in enumerate(WINDOWS):
        m_s = (m_ref[0, window], m_ref[1, window])
        att_s = (att_ref[0, window], att_ref[1, window])
        q_parts.append(dot3(cut(wks, ALL, span), m_s, NT))
        k_parts.append(dot3(cut(wqs, ALL, span), m_s, NN))
        v_parts.append(dot3(cut(fs, span, ALL), att_s, TN))
    gq = split(join(q_parts) - wq * d_ref[0:1])
    gk = split(join(k_parts) - wk * d_ref[1:2])
    gv = split(join(v_parts))
    p = split(dot3(gq, wqs, NT) + dot3(gk, wks, NT))
    r = split(dot3(gv, wvs, NT))
    both = tuple(jnp.concatenate([one, two], axis=0) for one, two in zip(p, r))
    tokens = x_ref.shape[0]
    step = tokens // 4
    copies = []
    for k in range(4):
        piece = pl.ds(k * step, step)
        xs, us = split(x_ref[piece]), split(u_ref[piece])
        token = tuple(jnp.concatenate([one, two], axis=1) for one, two in zip(xs, us))
        out_ref[piece] = dot3(token, both, NN)
        copy = pltpu.make_async_copy(out_ref.at[piece], out_hbm.at[piece], sems.at[k])
        copy.start()
        copies.append(copy)
    for copy in copies:
        copy.wait()


def total_kernel(own_ref, one_ref, two_ref, three_ref, mixer_ref, output_ref, sharp_ref):
    total = (own_ref[...] + two_ref[...]) + (one_ref[...] + three_ref[...])
    mixer_ref[...] = total[:ROWS, : 3 * D]
    output_ref[...] = total[:ROWS, 3 * D : 4 * D]
    sharp_ref[...] = total[0:1, 4 * D : 4 * D + VIEWS]


smem = pl.BlockSpec(memory_space=pltpu.SMEM)
vmem = pl.BlockSpec(memory_space=pltpu.VMEM)
hbm = pl.BlockSpec(memory_space=pltpu.HBM)


def call(kernel, ins, outs, shapes, scratch=(), flops=0, limit=32):
    return pl.pallas_call(
        kernel,
        in_specs=ins,
        out_specs=outs,
        out_shape=[jax.ShapeDtypeStruct(*one) for one in shapes],
        scratch_shapes=list(scratch),
        compiler_params=pltpu.CompilerParams(vmem_limit_bytes=limit * 1024 * 1024),
        cost_estimate=pl.CostEstimate(flops=flops, bytes_accessed=4 * 1024 * 1024, transcendentals=0),
    )


def body(
    incoming_embeddings,
    stacked_projector,
    final_projector,
    sharpness_per_view,
    upstream_sensitivity,
):
    x = incoming_embeddings[0]
    u = upstream_sensitivity[0]
    tokens = x.shape[0]
    core, chip = lax.axis_index("core"), lax.axis_index("x")
    ctx = (chip * Z_CHIPS + lax.axis_index("z")) * CORES + core
    place = jnp.stack([core, ctx * ROWS, chip]).astype(jnp.int32)
    unit = 2 * 3 * D * D * D

    half = ((HALF, T), f32)
    keep, send = call(
        gram_kernel,
        [smem, hbm, hbm],
        [vmem] * 2,
        [half] * 2,
        [
            pltpu.VMEM((tokens, D), f32),
            pltpu.VMEM((tokens, D), f32),
            pltpu.VMEM((CORES, X_CHIPS, 2, T, T), f32),
            pltpu.SemaphoreType.DMA((8,)),
        ],
        flops=6 * unit,
        limit=56,
    )(place, x, u)

    def swap(array):
        return lax.ppermute(array, "core", [(0, 1), (1, 0)])

    def shift(array, axis, by):
        size = lax.axis_size(axis)
        return lax.ppermute(array, axis, [(i, (i + by) % size) for i in range(size)])

    part = (keep + swap(send)).reshape(X_CHIPS, QUARTER, T)
    others = [shift(part[k], "x", k) for k in range(1, X_CHIPS)]
    part = part[0] + others[0] + others[1] + others[2]
    part = lax.all_to_all(part.reshape(Z_CHIPS, -1, T), "z", 0, 0, tiled=True).sum(axis=0)
    part = jnp.broadcast_to(part, (Z_CHIPS,) + part.shape)
    part = lax.all_to_all(part, "z", 0, 0, tiled=True).reshape(QUARTER, T)
    mine = jnp.concatenate([part] + [shift(part, "x", k) for k in range(1, X_CHIPS)])
    other = swap(mine)

    windows = ((2, 2, W, W), bf16)
    att, m, diagonal, rows = call(
        solve_kernel,
        [smem, smem] + [vmem] * 4,
        [vmem] * 4,
        [windows, windows, ((2, D), f32), ((8, 4 * D + T), f32)],
        [
            pltpu.VMEM((CORES, X_CHIPS, 2, T, T), f32),
            pltpu.VMEM((D, D), f32),
            pltpu.VMEM((D, D), f32),
        ],
        flops=8 * unit,
    )(place, sharpness_per_view, mine, other, stacked_projector, final_projector)

    others = [shift(rows, "dp", k) for k in range(1, lax.axis_size("dp"))]
    (input_grad,) = call(
        output_kernel,
        [vmem] * 7,
        [hbm],
        [((tokens, D), f32)],
        [pltpu.VMEM((tokens, D), f32), pltpu.SemaphoreType.DMA((4,))],
        flops=12 * unit,
    )(x, u, stacked_projector, final_projector, att, m, diagonal)
    mixer_grad, output_grad, sharpness_grad = call(
        total_kernel,
        [vmem] * 4,
        [vmem] * 3,
        [((ROWS, 3 * D), f32), ((ROWS, D), f32), ((1, VIEWS), f32)],
    )(rows, *others)
    return input_grad[None], mixer_grad, output_grad, sharpness_grad.reshape(VIEWS)


def solution(mesh):
    slides = mesh.shape["dp"]
    fine = Mesh(
        mesh.devices.reshape(slides, X_CHIPS, Z_CHIPS, CORES), ("dp", "x", "z", "core")
    )
    ctx = ("x", "z", "core")
    return jax.shard_map(
        body,
        mesh=fine,
        in_specs=(P("dp", ctx, None), P(), P(), P(), P("dp", ctx, None)),
        out_specs=(P("dp", ctx, None), P(ctx, None), P(ctx, None), P()),
        check_vma=False,
    )
```

```python
import functools
import math

import jax
import jax.numpy as jnp
from jax import lax
from jax.experimental import pallas as pl
from jax.experimental.pallas import tpu as pltpu
from jax.sharding import Mesh, PartitionSpec as P

epsilon = 1e-06
D = 384
VIEWS = 8
HEAD = D // VIEWS
T = 128
W = 256
X_CHIPS, Z_CHIPS, CORES = 4, 8, 2
SHARES = X_CHIPS * Z_CHIPS
ROWS = D // (SHARES * CORES)
HALF = 8 * T
QUARTER = HALF // X_CHIPS
PICK = 16
BLOCKS = [("a", i, j) for i in range(3) for j in range(i, 3)]
BLOCKS += [("b", i, j) for i in range(3) for j in range(3)]


def place_of(at):
    return at // 8, at % 8 // 2, at % 2


f32, bf16 = jnp.float32, jnp.bfloat16
NN = ((1,), (0,))
NT = ((1,), (1,))
TN = ((0,), (0,))


def split(a):
    high = a.astype(bf16)
    return high, (a - high.astype(f32)).astype(bf16)


def dot3(a, b, dims):
    (ca,), (cb,) = dims
    return lax.dot_general(
        jnp.concatenate([a[0], a[0], a[1]], axis=ca),
        jnp.concatenate([b[0], b[1], b[0]], axis=cb),
        (dims, ((), ())),
        preferred_element_type=f32,
    )


def row_dot3(a, b, dims):
    d = functools.partial(
        lax.dot_general, dimension_numbers=(dims, ((), ())), preferred_element_type=f32
    )
    both = d(jnp.concatenate(a, axis=0), b[0])
    return both[:PICK] + both[PICK:] + d(a[0], b[1])


def cut(pair, rows, cols):
    return pair[0][rows, cols], pair[1][rows, cols]


ALL = slice(None)
WINDOWS = (slice(0, W), slice(D - W, D))


def join(parts):
    one, two = parts
    return jnp.concatenate([one[:, :T], one[:, T:] + two[:, :T], two[:, T:]], axis=1)


def gram_kernel(place_ref, x_hbm, u_hbm, keep_ref, send_ref, x_ref, u_ref, pay_ref, sems):
    tokens = x_ref.shape[0]
    step = tokens // 4
    copies = []
    for at, (source, target) in enumerate(((x_hbm, x_ref), (u_hbm, u_ref))):
        for k in range(4):
            piece = pl.ds(k * step, step)
            copy = pltpu.make_async_copy(source.at[piece], target.at[piece], sems.at[at * 4 + k])
            copy.start()
            copies.append(copy)
    for copy in copies[:4]:
        copy.wait()
    d = functools.partial(
        lax.dot_general, dimension_numbers=(TN, ((), ())), preferred_element_type=f32
    )
    xh, xl = split(x_ref[...])
    cross = d(xh, xl)
    grams = {"a": d(xh, xh) + cross + cross.T}
    for copy in copies[4:]:
        copy.wait()
    uh, ul = split(u_ref[...])
    grams["b"] = d(xh, uh) + (d(xh, ul) + d(xl, uh))
    for at, (name, i, j) in enumerate(BLOCKS):
        pay_ref[place_of(at)] = grams[name][i * T : (i + 1) * T, j * T : (j + 1) * T]
    pay_ref[place_of(15)] = jnp.zeros((T, T), f32)
    core, chip = place_ref[0], place_ref[2]
    for k in range(X_CHIPS):
        to = lax.rem(chip + k, X_CHIPS)
        piece = pl.ds(k * QUARTER, QUARTER)
        keep_ref[piece] = pay_ref[core, to].reshape(QUARTER, T)
        send_ref[piece] = pay_ref[1 - core, to].reshape(QUARTER, T)


def heads_of(shape, axis, window):
    feature = lax.broadcasted_iota(jnp.int32, shape, axis) + window * (D - W)
    head = jnp.zeros(shape, jnp.int32)
    for h in range(1, VIEWS):
        head = head + jnp.where(feature >= h * HEAD, 1, 0)
    return feature, head


def masks(window):
    _, rows = heads_of((W, W), 0, window)
    _, cols = heads_of((W, W), 1, window)
    own = (rows < VIEWS // 2) if window == 0 else (rows >= VIEWS // 2)
    return (rows == cols) & own


def eye_of(size):
    return lax.broadcasted_iota(jnp.int32, (size, size), 0) == lax.broadcasted_iota(
        jnp.int32, (size, size), 1
    )


def to_col(eye, v):
    return jnp.sum(jnp.where(eye, v, 0.0), axis=1, keepdims=True)


def to_row(eye, v):
    return jnp.sum(jnp.where(eye, v, 0.0), axis=0, keepdims=True)


def sharp_col(sharp_ref, window):
    _, head = heads_of((W, 1), 0, window)
    sharp = jnp.zeros((W, 1), f32)
    for h in range(VIEWS):
        sharp = jnp.where(head == h, sharp_ref[h], sharp)
    return sharp


def rows_of(first, load, size):
    base = jnp.minimum(first // 8 * 8, size - PICK)
    block = load(pl.ds(pl.multiple_of(base, 8), PICK))
    return pltpu.roll(block, PICK - (first - base), 0)


scale = 1.0 / math.sqrt(262144)


def solve_kernel(
    place_ref, sharp_ref, w_ref, f_ref, m0, m1, m2, m3, o0, o1, o2, o3,
    gv_ref, m_ref, d_ref, rows_ref, block_ref, a_ref, b_ref, c_ref, t_ref, att_ref,
):
    core, first, chip = place_ref[0], place_ref[1], place_ref[2]
    for k in range(X_CHIPS):
        origin = lax.rem(chip + X_CHIPS - k, X_CHIPS)
        block_ref[core, origin] = (m0, m1, m2, m3)[k][...].reshape(2, T, T)
        block_ref[1 - core, origin] = (o0, o1, o2, o3)[k][...].reshape(2, T, T)
    for at, (name, i, j) in enumerate(BLOCKS):
        block = block_ref[place_of(at)]
        ref = a_ref if name == "a" else b_ref
        ref[i * T : (i + 1) * T, j * T : (j + 1) * T] = block
        if name == "a" and i != j:
            ref[j * T : (j + 1) * T, i * T : (i + 1) * T] = block.T
    a_s, b_s = split(a_ref[...]), split(b_ref[...])
    ws, fs = split(w_ref[...]), split(f_ref[...])
    t = dot3(a_s, cut(ws, ALL, slice(0, 2 * D)), NN)
    t_ref[...] = t
    c = dot3(cut(ws, ALL, slice(2 * D, 3 * D)), b_s, TN)
    c_ref[...] = c
    c_s = split(c)
    square = jnp.sum(w_ref[:, : 2 * D] * t, axis=0, keepdims=True)
    inverse = lax.rsqrt(jnp.maximum(square, 0.0) + epsilon)
    q_inv, k_inv = inverse[:, :D], inverse[:, D:]
    tks = split(t[:, D:])
    t_rows = rows_of(first, lambda rows: t_ref[rows], D)
    b_rows = rows_of(first, lambda rows: b_ref[rows], D)
    tq_rows, tk_rows = split(t_rows[:, :D]), split(t_rows[:, D:])
    eye = eye_of(W)
    attentions, covs, mixers = [], [], []
    for window, span in enumerate(WINDOWS):
        same = masks(window)
        cov = dot3(cut(ws, ALL, span), cut(tks, ALL, span), TN)
        cov = jnp.where(same, cov * to_col(eye, q_inv[:, span]) * k_inv[:, span], 0.0)
        table = jnp.where(same, jnp.exp(sharp_col(sharp_ref, window) * cov), 0.0)
        total = jnp.sum(table, axis=1, keepdims=True)
        attention = table / jnp.where(total > 0.0, total, 1.0)
        att_ref[window] = attention
        attentions.append(attention)
        covs.append(cov)
        mixers.append(dot3(cut(fs, span, ALL), split(attention), TN))
    gv = split(join(mixers))
    gv_ref[0], gv_ref[1] = gv
    window = jnp.where(first >= D // 2, 1, 0)
    offset = pl.multiple_of(window * (D - W), T)
    att_rows = rows_of(first - offset, lambda rows: att_ref[window, rows], W)
    c_part = split(c_ref[pl.ds(offset, W)])
    rows_ref[:, 2 * D : 3 * D] = row_dot3(split(b_rows), gv, NN)[:8] * scale
    rows_ref[:, 3 * D : 4 * D] = row_dot3(split(att_rows), c_part, NN)[:8] * scale
    q_sum, k_sum, q_rows, k_rows = [], [], [], []
    temp = jnp.zeros((1, T), f32)
    for window, span in enumerate(WINDOWS):
        attention, cov = attentions[window], covs[window]
        sharp = sharp_col(sharp_ref, window)
        attention_grad = dot3(cut(fs, span, ALL), cut(c_s, span, ALL), NT)
        inner = jnp.sum(attention * attention_grad, axis=1, keepdims=True)
        score_grad = attention * (attention_grad - inner)
        weighed = score_grad * cov
        by_feature = jnp.sum(weighed, axis=1, keepdims=True)
        q_sum.append(to_row(eye, sharp * by_feature))
        k_sum.append(jnp.sum(sharp * weighed, axis=0, keepdims=True))
        m_s = split(sharp * score_grad * to_col(eye, q_inv[:, span]) * k_inv[:, span])
        m_ref[0, window], m_ref[1, window] = m_s
        q_rows.append(row_dot3(cut(tk_rows, ALL, span), m_s, NT))
        k_rows.append(row_dot3(cut(tq_rows, ALL, span), m_s, NN))
        _, head = heads_of((W, T), 0, window)
        lane = lax.broadcasted_iota(jnp.int32, (W, T), 1)
        temp += jnp.sum(jnp.where(head == lane, by_feature, 0.0), axis=0, keepdims=True)
    d_q = join(q_sum) * (q_inv * q_inv)
    d_k = join(k_sum) * (k_inv * k_inv)
    d_ref[0:1] = d_q
    d_ref[1:2] = d_k
    rows_ref[:, :D] = (join(q_rows) - t_rows[:, :D] * d_q)[:8] * scale
    rows_ref[:, D : 2 * D] = (join(k_rows) - t_rows[:, D:] * d_k)[:8] * scale
    rows_ref[:, 4 * D :] = jnp.broadcast_to(temp * scale, (8, T))


def output_kernel(
    x_ref, u_ref, w_ref, gv_ref, m_ref, d_ref, out_hbm, out_ref, sems
):
    ws = split(w_ref[...])
    q_parts, k_parts = [], []
    for window, span in enumerate(WINDOWS):
        m_s = (m_ref[0, window], m_ref[1, window])
        q_parts.append(dot3(cut(ws, ALL, slice(D + span.start, D + span.stop)), m_s, NT))
        k_parts.append(dot3(cut(ws, ALL, span), m_s, NN))
    gq = split(join(q_parts) - w_ref[:, :D] * d_ref[0:1])
    gk = split(join(k_parts) - w_ref[:, D : 2 * D] * d_ref[1:2])
    g = tuple(jnp.concatenate([one, two], axis=1) for one, two in zip(gq, gk))
    gv = (gv_ref[0], gv_ref[1])
    p = split(dot3(g, cut(ws, ALL, slice(0, 2 * D)), NT))
    r = split(dot3(gv, cut(ws, ALL, slice(2 * D, 3 * D)), NT))
    factors = tuple(jnp.concatenate([one, two], axis=0) for one, two in zip(p, r))
    tokens = x_ref.shape[0]
    step = tokens // 8
    copies = []
    for k in range(8):
        piece = pl.ds(k * step, step)
        xs, us = split(x_ref[piece]), split(u_ref[piece])
        token = tuple(jnp.concatenate([one, two], axis=1) for one, two in zip(xs, us))
        out_ref[piece] = dot3(token, factors, NN)
        copy = pltpu.make_async_copy(out_ref.at[piece], out_hbm.at[piece], sems.at[k])
        copy.start()
        copies.append(copy)
    for copy in copies:
        copy.wait()


def total_kernel(own_ref, one_ref, two_ref, three_ref, mixer_ref, output_ref, sharp_ref):
    total = (own_ref[...] + two_ref[...]) + (one_ref[...] + three_ref[...])
    mixer_ref[...] = total[:ROWS, : 3 * D]
    output_ref[...] = total[:ROWS, 3 * D : 4 * D]
    sharp_ref[...] = total[0:1, 4 * D : 4 * D + VIEWS]


smem = pl.BlockSpec(memory_space=pltpu.SMEM)
vmem = pl.BlockSpec(memory_space=pltpu.VMEM)
hbm = pl.BlockSpec(memory_space=pltpu.HBM)


def call(kernel, ins, outs, shapes, scratch=(), flops=0, limit=32):
    return pl.pallas_call(
        kernel,
        in_specs=ins,
        out_specs=outs,
        out_shape=[jax.ShapeDtypeStruct(*one) for one in shapes],
        scratch_shapes=list(scratch),
        compiler_params=pltpu.CompilerParams(vmem_limit_bytes=limit * 1024 * 1024),
        cost_estimate=pl.CostEstimate(flops=flops, bytes_accessed=4 * 1024 * 1024, transcendentals=0),
    )


def body(
    incoming_embeddings,
    stacked_projector,
    final_projector,
    sharpness_per_view,
    upstream_sensitivity,
):
    x = incoming_embeddings[0]
    u = upstream_sensitivity[0]
    tokens = x.shape[0]
    core, chip = lax.axis_index("core"), lax.axis_index("x")
    ctx = (chip * Z_CHIPS + lax.axis_index("z")) * CORES + core
    place = jnp.stack([core, ctx * ROWS, chip]).astype(jnp.int32)
    unit = 2 * 3 * D * D * D

    def in_hbm(array):
        return pltpu.with_memory_space_constraint(array, pltpu.HBM)

    half = ((HALF, T), f32)
    keep, send = call(
        gram_kernel,
        [smem, hbm, hbm],
        [vmem] * 2,
        [half] * 2,
        [
            pltpu.VMEM((tokens, D), f32),
            pltpu.VMEM((tokens, D), f32),
            pltpu.VMEM((CORES, X_CHIPS, 2, T, T), f32),
            pltpu.SemaphoreType.DMA((8,)),
        ],
        flops=6 * unit,
    )(place, in_hbm(x), in_hbm(u))

    def swap(array):
        return lax.ppermute(array, "core", [(0, 1), (1, 0)])

    def shift(array, axis, by):
        size = lax.axis_size(axis)
        return lax.ppermute(array, axis, [(i, (i + by) % size) for i in range(size)])

    part = (keep + swap(send)).reshape(X_CHIPS, QUARTER, T)
    others = [shift(part[k], "x", k) for k in range(1, X_CHIPS)]
    part = part[0] + others[0] + others[1] + others[2]
    part = lax.all_to_all(part.reshape(Z_CHIPS, -1, T), "z", 0, 0, tiled=True).sum(axis=0)
    part = jnp.broadcast_to(part, (Z_CHIPS,) + part.shape)
    part = lax.all_to_all(part, "z", 0, 0, tiled=True).reshape(QUARTER, T)
    mine = [part] + [shift(part, "x", k) for k in range(1, X_CHIPS)]
    other = [swap(piece) for piece in mine]

    gv, m, diagonal, rows = call(
        solve_kernel,
        [smem, smem] + [vmem] * 10,
        [vmem] * 4,
        [((2, D, D), bf16), ((2, 2, W, W), bf16), ((2, D), f32), ((8, 4 * D + T), f32)],
        [
            pltpu.VMEM((CORES, X_CHIPS, 2, T, T), f32),
            pltpu.VMEM((D, D), f32),
            pltpu.VMEM((D, D), f32),
            pltpu.VMEM((D, D), f32),
            pltpu.VMEM((D, 2 * D), f32),
            pltpu.VMEM((2, W, W), f32),
        ],
        flops=8 * unit,
    )(place, sharpness_per_view, stacked_projector, final_projector, *mine, *other)

    one, two, three = [shift(rows, "dp", k) for k in range(1, lax.axis_size("dp"))]
    (input_grad,) = call(
        output_kernel,
        [vmem] * 6,
        [hbm],
        [((tokens, D), f32)],
        [pltpu.VMEM((tokens, D), f32), pltpu.SemaphoreType.DMA((8,))],
        flops=12 * unit,
    )(x, u, stacked_projector, gv, m, diagonal)
    mixer_grad, output_grad, sharpness_grad = call(
        total_kernel,
        [vmem] * 4,
        [vmem] * 3,
        [((ROWS, 3 * D), f32), ((ROWS, D), f32), ((1, VIEWS), f32)],
    )(rows, one, two, three)
    return input_grad[None], mixer_grad, output_grad, sharpness_grad.reshape(VIEWS)


def solution(mesh):
    slides = mesh.shape["dp"]
    fine = Mesh(
        mesh.devices.reshape(slides, X_CHIPS, Z_CHIPS, CORES), ("dp", "x", "z", "core")
    )
    ctx = ("x", "z", "core")
    return jax.shard_map(
        body,
        mesh=fine,
        in_specs=(P("dp", ctx, None), P(), P(), P(), P("dp", ctx, None)),
        out_specs=(P("dp", ctx, None), P(ctx, None), P(ctx, None), P()),
        check_vma=False,
    )
```

```python
import functools
import math

import jax
import jax.numpy as jnp
from jax import lax
from jax.experimental import pallas as pl
from jax.experimental.pallas import tpu as pltpu
from jax.sharding import Mesh, PartitionSpec as P

epsilon = 1e-06
D = 384
VIEWS = 8
HEAD = D // VIEWS
T = 128
W = 256
X_CHIPS, Z_CHIPS, CORES = 4, 8, 2
SHARES = X_CHIPS * Z_CHIPS
ROWS = D // (SHARES * CORES)
HALF = 8 * T
QUARTER = HALF // X_CHIPS
PICK = 16
BLOCKS = [("a", i, j) for i in range(3) for j in range(i, 3)]
BLOCKS += [("b", i, j) for i in range(3) for j in range(3)]


def place_of(at):
    return at // 8, at % 8 // 2, at % 2


f32, bf16 = jnp.float32, jnp.bfloat16
NN = ((1,), (0,))
NT = ((1,), (1,))
TN = ((0,), (0,))


def split(a):
    high = a.astype(bf16)
    return high, (a - high.astype(f32)).astype(bf16)


def dot3(a, b, dims):
    (ca,), (cb,) = dims
    return lax.dot_general(
        jnp.concatenate([a[0], a[0], a[1]], axis=ca),
        jnp.concatenate([b[0], b[1], b[0]], axis=cb),
        (dims, ((), ())),
        preferred_element_type=f32,
    )


def row_dot3(a, b, dims):
    d = functools.partial(
        lax.dot_general, dimension_numbers=(dims, ((), ())), preferred_element_type=f32
    )
    both = d(jnp.concatenate(a, axis=0), b[0])
    return both[:PICK] + both[PICK:] + d(a[0], b[1])


def cut(pair, rows, cols):
    return pair[0][rows, cols], pair[1][rows, cols]


ALL = slice(None)
WINDOWS = (slice(0, W), slice(D - W, D))


def join(parts):
    one, two = parts
    return jnp.concatenate([one[:, :T], one[:, T:] + two[:, :T], two[:, T:]], axis=1)


def gram_kernel(place_ref, x_hbm, u_hbm, keep_ref, send_ref, x_ref, u_ref, pay_ref, sems):
    tokens = x_ref.shape[0]
    step = tokens // 4
    copies = []
    for at, (source, target) in enumerate(((x_hbm, x_ref), (u_hbm, u_ref))):
        for k in range(4):
            piece = pl.ds(k * step, step)
            copy = pltpu.make_async_copy(source.at[piece], target.at[piece], sems.at[at * 4 + k])
            copy.start()
            copies.append(copy)
    for copy in copies[:4]:
        copy.wait()
    d = functools.partial(
        lax.dot_general, dimension_numbers=(TN, ((), ())), preferred_element_type=f32
    )
    xh, xl = split(x_ref[...])
    cross = d(xh, xl)
    grams = {"a": d(xh, xh) + cross + cross.T}
    for copy in copies[4:]:
        copy.wait()
    uh, ul = split(u_ref[...])
    grams["b"] = d(xh, uh) + (d(xh, ul) + d(xl, uh))
    for at, (name, i, j) in enumerate(BLOCKS):
        pay_ref[place_of(at)] = grams[name][i * T : (i + 1) * T, j * T : (j + 1) * T]
    pay_ref[place_of(15)] = jnp.zeros((T, T), f32)
    core, chip = place_ref[0], place_ref[2]
    for k in range(X_CHIPS):
        to = lax.rem(chip + k, X_CHIPS)
        piece = pl.ds(k * QUARTER, QUARTER)
        keep_ref[piece] = pay_ref[core, to].reshape(QUARTER, T)
        send_ref[piece] = pay_ref[1 - core, to].reshape(QUARTER, T)


def heads_of(shape, axis, window):
    feature = lax.broadcasted_iota(jnp.int32, shape, axis) + window * (D - W)
    head = jnp.zeros(shape, jnp.int32)
    for h in range(1, VIEWS):
        head = head + jnp.where(feature >= h * HEAD, 1, 0)
    return feature, head


def masks(window):
    _, rows = heads_of((W, W), 0, window)
    _, cols = heads_of((W, W), 1, window)
    own = (rows < VIEWS // 2) if window == 0 else (rows >= VIEWS // 2)
    return (rows == cols) & own


def eye_of(size):
    return lax.broadcasted_iota(jnp.int32, (size, size), 0) == lax.broadcasted_iota(
        jnp.int32, (size, size), 1
    )


def to_col(eye, v):
    return jnp.sum(jnp.where(eye, v, 0.0), axis=1, keepdims=True)


def to_row(eye, v):
    return jnp.sum(jnp.where(eye, v, 0.0), axis=0, keepdims=True)


def sharp_col(sharp_ref, window):
    _, head = heads_of((W, 1), 0, window)
    sharp = jnp.zeros((W, 1), f32)
    for h in range(VIEWS):
        sharp = jnp.where(head == h, sharp_ref[h], sharp)
    return sharp


def rows_of(first, load, size):
    base = jnp.minimum(first // 8 * 8, size - PICK)
    block = load(pl.ds(pl.multiple_of(base, 8), PICK))
    return pltpu.roll(block, PICK - (first - base), 0)


scale = 1.0 / math.sqrt(262144)


def solve_kernel(
    place_ref, sharp_ref, w_ref, f_ref, m0, m1, m2, m3, o0, o1, o2, o3,
    gv_ref, m_ref, d_ref, rows_ref, block_ref, a_ref, b_ref, c_ref, t_ref, att_ref,
):
    core, first, chip = place_ref[0], place_ref[1], place_ref[2]
    for k in range(X_CHIPS):
        origin = lax.rem(chip + X_CHIPS - k, X_CHIPS)
        block_ref[core, origin] = (m0, m1, m2, m3)[k][...].reshape(2, T, T)
        block_ref[1 - core, origin] = (o0, o1, o2, o3)[k][...].reshape(2, T, T)
    for at, (name, i, j) in enumerate(BLOCKS):
        block = block_ref[place_of(at)]
        ref = a_ref if name == "a" else b_ref
        ref[i * T : (i + 1) * T, j * T : (j + 1) * T] = block
        if name == "a" and i != j:
            ref[j * T : (j + 1) * T, i * T : (i + 1) * T] = block.T
    a_s, b_s = split(a_ref[...]), split(b_ref[...])
    ws, fs = split(w_ref[...]), split(f_ref[...])
    t = dot3(a_s, cut(ws, ALL, slice(0, 2 * D)), NN)
    t_ref[...] = t
    c = dot3(cut(ws, ALL, slice(2 * D, 3 * D)), b_s, TN)
    c_ref[...] = c
    c_s = split(c)
    square = jnp.sum(w_ref[:, : 2 * D] * t, axis=0, keepdims=True)
    inverse = lax.rsqrt(jnp.maximum(square, 0.0) + epsilon)
    q_inv, k_inv = inverse[:, :D], inverse[:, D:]
    tks = split(t[:, D:])
    t_rows = rows_of(first, lambda rows: t_ref[rows], D)
    b_rows = rows_of(first, lambda rows: b_ref[rows], D)
    tq_rows, tk_rows = split(t_rows[:, :D]), split(t_rows[:, D:])
    eye = eye_of(W)
    attentions, covs, mixers = [], [], []
    for window, span in enumerate(WINDOWS):
        same = masks(window)
        cov = dot3(cut(ws, ALL, span), cut(tks, ALL, span), TN)
        cov = jnp.where(same, cov * to_col(eye, q_inv[:, span]) * k_inv[:, span], 0.0)
        table = jnp.where(same, jnp.exp(sharp_col(sharp_ref, window) * cov), 0.0)
        total = jnp.sum(table, axis=1, keepdims=True)
        attention = table / jnp.where(total > 0.0, total, 1.0)
        att_ref[window] = attention
        attentions.append(attention)
        covs.append(cov)
        mixers.append(dot3(cut(fs, span, ALL), split(attention), TN))
    gv = split(join(mixers))
    gv_ref[0], gv_ref[1] = gv
    window = jnp.where(first >= D // 2, 1, 0)
    offset = pl.multiple_of(window * (D - W), T)
    att_rows = rows_of(first - offset, lambda rows: att_ref[window, rows], W)
    c_part = split(c_ref[pl.ds(offset, W)])
    rows_ref[:, 2 * D : 3 * D] = row_dot3(split(b_rows), gv, NN)[:8] * scale
    rows_ref[:, 3 * D : 4 * D] = row_dot3(split(att_rows), c_part, NN)[:8] * scale
    q_sum, k_sum, q_rows, k_rows = [], [], [], []
    temp = jnp.zeros((1, T), f32)
    for window, span in enumerate(WINDOWS):
        attention, cov = attentions[window], covs[window]
        sharp = sharp_col(sharp_ref, window)
        attention_grad = dot3(cut(fs, span, ALL), cut(c_s, span, ALL), NT)
        inner = jnp.sum(attention * attention_grad, axis=1, keepdims=True)
        score_grad = attention * (attention_grad - inner)
        weighed = score_grad * cov
        by_feature = jnp.sum(weighed, axis=1, keepdims=True)
        q_sum.append(to_row(eye, sharp * by_feature))
        k_sum.append(jnp.sum(sharp * weighed, axis=0, keepdims=True))
        m_s = split(sharp * score_grad * to_col(eye, q_inv[:, span]) * k_inv[:, span])
        m_ref[0, window], m_ref[1, window] = m_s
        q_rows.append(row_dot3(cut(tk_rows, ALL, span), m_s, NT))
        k_rows.append(row_dot3(cut(tq_rows, ALL, span), m_s, NN))
        _, head = heads_of((W, T), 0, window)
        lane = lax.broadcasted_iota(jnp.int32, (W, T), 1)
        temp += jnp.sum(jnp.where(head == lane, by_feature, 0.0), axis=0, keepdims=True)
    d_q = join(q_sum) * (q_inv * q_inv)
    d_k = join(k_sum) * (k_inv * k_inv)
    d_ref[0:1] = d_q
    d_ref[1:2] = d_k
    rows_ref[:, :D] = (join(q_rows) - t_rows[:, :D] * d_q)[:8] * scale
    rows_ref[:, D : 2 * D] = (join(k_rows) - t_rows[:, D:] * d_k)[:8] * scale
    rows_ref[:, 4 * D :] = jnp.broadcast_to(temp * scale, (8, T))


def output_kernel(
    x_ref, u_ref, w_ref, gv_ref, m_ref, d_ref, out_hbm, out_ref, sems
):
    ws = split(w_ref[...])
    q_parts, k_parts = [], []
    for window, span in enumerate(WINDOWS):
        m_s = (m_ref[0, window], m_ref[1, window])
        q_parts.append(dot3(cut(ws, ALL, slice(D + span.start, D + span.stop)), m_s, NT))
        k_parts.append(dot3(cut(ws, ALL, span), m_s, NN))
    gq = split(join(q_parts) - w_ref[:, :D] * d_ref[0:1])
    gk = split(join(k_parts) - w_ref[:, D : 2 * D] * d_ref[1:2])
    g = tuple(jnp.concatenate([one, two], axis=1) for one, two in zip(gq, gk))
    gv = (gv_ref[0], gv_ref[1])
    p = split(dot3(g, cut(ws, ALL, slice(0, 2 * D)), NT))
    r = split(dot3(gv, cut(ws, ALL, slice(2 * D, 3 * D)), NT))
    factors = tuple(jnp.concatenate([one, two], axis=0) for one, two in zip(p, r))
    tokens = x_ref.shape[0]
    step = tokens // 8
    copies = []
    for k in range(8):
        piece = pl.ds(k * step, step)
        xs, us = split(x_ref[piece]), split(u_ref[piece])
        token = tuple(jnp.concatenate([one, two], axis=1) for one, two in zip(xs, us))
        out_ref[piece] = dot3(token, factors, NN)
        copy = pltpu.make_async_copy(out_ref.at[piece], out_hbm.at[piece], sems.at[k])
        copy.start()
        copies.append(copy)
    for copy in copies:
        copy.wait()


def total_kernel(own_ref, one_ref, two_ref, three_ref, mixer_ref, output_ref, sharp_ref):
    total = (own_ref[...] + two_ref[...]) + (one_ref[...] + three_ref[...])
    mixer_ref[...] = total[:ROWS, : 3 * D]
    output_ref[...] = total[:ROWS, 3 * D : 4 * D]
    sharp_ref[...] = total[0:1, 4 * D : 4 * D + VIEWS]


smem = pl.BlockSpec(memory_space=pltpu.SMEM)
vmem = pl.BlockSpec(memory_space=pltpu.VMEM)
hbm = pl.BlockSpec(memory_space=pltpu.HBM)


def call(kernel, ins, outs, shapes, scratch=(), flops=0, limit=32):
    return pl.pallas_call(
        kernel,
        in_specs=ins,
        out_specs=outs,
        out_shape=[jax.ShapeDtypeStruct(*one) for one in shapes],
        scratch_shapes=list(scratch),
        compiler_params=pltpu.CompilerParams(vmem_limit_bytes=limit * 1024 * 1024),
        cost_estimate=pl.CostEstimate(flops=flops, bytes_accessed=4 * 1024 * 1024, transcendentals=0),
    )


def body(
    incoming_embeddings,
    stacked_projector,
    final_projector,
    sharpness_per_view,
    upstream_sensitivity,
):
    x = incoming_embeddings[0]
    u = upstream_sensitivity[0]
    tokens = x.shape[0]
    core, chip = lax.axis_index("core"), lax.axis_index("x")
    ctx = (chip * Z_CHIPS + lax.axis_index("z")) * CORES + core
    place = jnp.stack([core, ctx * ROWS, chip]).astype(jnp.int32)
    unit = 2 * 3 * D * D * D

    def in_hbm(array):
        return pltpu.with_memory_space_constraint(array, pltpu.HBM)

    half = ((HALF, T), f32)
    keep, send = call(
        gram_kernel,
        [smem, hbm, hbm],
        [vmem] * 2,
        [half] * 2,
        [
            pltpu.VMEM((tokens, D), f32),
            pltpu.VMEM((tokens, D), f32),
            pltpu.VMEM((CORES, X_CHIPS, 2, T, T), f32),
            pltpu.SemaphoreType.DMA((8,)),
        ],
        flops=6 * unit,
    )(place, in_hbm(x), in_hbm(u))

    def swap(array):
        return lax.ppermute(array, "core", [(0, 1), (1, 0)])

    def shift(array, axis, by):
        size = lax.axis_size(axis)
        return lax.ppermute(array, axis, [(i, (i + by) % size) for i in range(size)])

    part = (keep + swap(send)).reshape(X_CHIPS, QUARTER, T)
    others = [shift(part[k], "x", k) for k in range(1, X_CHIPS)]
    part = part[0] + others[0] + others[1] + others[2]
    for apart in (4, 2, 1):
        part = part + lax.ppermute(part, "z", [(i, i ^ apart) for i in range(Z_CHIPS)])
    mine = [part] + [shift(part, "x", k) for k in range(1, X_CHIPS)]
    other = [swap(piece) for piece in mine]

    gv, m, diagonal, rows = call(
        solve_kernel,
        [smem, smem] + [vmem] * 10,
        [vmem] * 4,
        [((2, D, D), bf16), ((2, 2, W, W), bf16), ((2, D), f32), ((8, 4 * D + T), f32)],
        [
            pltpu.VMEM((CORES, X_CHIPS, 2, T, T), f32),
            pltpu.VMEM((D, D), f32),
            pltpu.VMEM((D, D), f32),
            pltpu.VMEM((D, D), f32),
            pltpu.VMEM((D, 2 * D), f32),
            pltpu.VMEM((2, W, W), f32),
        ],
        flops=8 * unit,
    )(place, sharpness_per_view, stacked_projector, final_projector, *mine, *other)

    one, two, three = [shift(rows, "dp", k) for k in range(1, lax.axis_size("dp"))]
    (input_grad,) = call(
        output_kernel,
        [vmem] * 6,
        [hbm],
        [((tokens, D), f32)],
        [pltpu.VMEM((tokens, D), f32), pltpu.SemaphoreType.DMA((8,))],
        flops=12 * unit,
    )(x, u, stacked_projector, gv, m, diagonal)
    mixer_grad, output_grad, sharpness_grad = call(
        total_kernel,
        [vmem] * 4,
        [vmem] * 3,
        [((ROWS, 3 * D), f32), ((ROWS, D), f32), ((1, VIEWS), f32)],
    )(rows, one, two, three)
    return input_grad[None], mixer_grad, output_grad, sharpness_grad.reshape(VIEWS)


def solution(mesh):
    slides = mesh.shape["dp"]
    fine = Mesh(
        mesh.devices.reshape(slides, X_CHIPS, Z_CHIPS, CORES), ("dp", "x", "z", "core")
    )
    ctx = ("x", "z", "core")
    return jax.shard_map(
        body,
        mesh=fine,
        in_specs=(P("dp", ctx, None), P(), P(), P(), P("dp", ctx, None)),
        out_specs=(P("dp", ctx, None), P(ctx, None), P(ctx, None), P()),
        check_vma=False,
    )
```

```python
import functools
import math

import jax
import jax.numpy as jnp
from jax import lax
from jax.experimental import pallas as pl
from jax.experimental.pallas import tpu as pltpu
from jax.sharding import Mesh, PartitionSpec as P

epsilon = 1e-06
D = 384
VIEWS = 8
HEAD = D // VIEWS
T = 128
W = 256
X_CHIPS, Z_CHIPS, CORES = 4, 8, 2
SHARES = X_CHIPS * Z_CHIPS
ROWS = D // (SHARES * CORES)
HALF = 8 * T
SQUARE = 4
AWAY = (3, 2, 1)
QUARTER = HALF // SQUARE
PICK = 16
BLOCKS = [("a", i, j) for i in range(3) for j in range(i, 3)]
BLOCKS += [("b", i, j) for i in range(3) for j in range(3)]


def place_of(at):
    return at // 8, at % 8 // 2, at % 2


f32, bf16 = jnp.float32, jnp.bfloat16
NN = ((1,), (0,))
NT = ((1,), (1,))
TN = ((0,), (0,))


def split(a):
    high = a.astype(bf16)
    return high, (a - high.astype(f32)).astype(bf16)


def dot3(a, b, dims):
    (ca,), (cb,) = dims
    return lax.dot_general(
        jnp.concatenate([a[0], a[0], a[1]], axis=ca),
        jnp.concatenate([b[0], b[1], b[0]], axis=cb),
        (dims, ((), ())),
        preferred_element_type=f32,
    )


def row_dot3(a, b, dims):
    d = functools.partial(
        lax.dot_general, dimension_numbers=(dims, ((), ())), preferred_element_type=f32
    )
    both = d(jnp.concatenate(a, axis=0), b[0])
    return both[:PICK] + both[PICK:] + d(a[0], b[1])


def cut(pair, rows, cols):
    return pair[0][rows, cols], pair[1][rows, cols]


ALL = slice(None)
WINDOWS = (slice(0, W), slice(D - W, D))


def join(parts):
    one, two = parts
    return jnp.concatenate([one[:, :T], one[:, T:] + two[:, :T], two[:, T:]], axis=1)


def gram_kernel(place_ref, x_hbm, u_hbm, keep_ref, send_ref, x_ref, u_ref, pay_ref, sems):
    tokens = x_ref.shape[0]
    step = tokens // 4
    copies = []
    for at, (source, target) in enumerate(((x_hbm, x_ref), (u_hbm, u_ref))):
        for k in range(4):
            piece = pl.ds(k * step, step)
            copy = pltpu.make_async_copy(source.at[piece], target.at[piece], sems.at[at * 4 + k])
            copy.start()
            copies.append(copy)
    for copy in copies[:4]:
        copy.wait()
    d = functools.partial(
        lax.dot_general, dimension_numbers=(TN, ((), ())), preferred_element_type=f32
    )
    xh, xl = split(x_ref[...])
    cross = d(xh, xl)
    grams = {"a": d(xh, xh) + cross + cross.T}
    for copy in copies[4:]:
        copy.wait()
    uh, ul = split(u_ref[...])
    grams["b"] = d(xh, uh) + (d(xh, ul) + d(xl, uh))
    for at, (name, i, j) in enumerate(BLOCKS):
        pay_ref[place_of(at)] = grams[name][i * T : (i + 1) * T, j * T : (j + 1) * T]
    pay_ref[place_of(15)] = jnp.zeros((T, T), f32)
    core, chip = place_ref[0], place_ref[2]
    for k in range(SQUARE):
        to = chip ^ k
        piece = pl.ds(k * QUARTER, QUARTER)
        keep_ref[piece] = pay_ref[core, to].reshape(QUARTER, T)
        send_ref[piece] = pay_ref[1 - core, to].reshape(QUARTER, T)


def heads_of(shape, axis, window):
    feature = lax.broadcasted_iota(jnp.int32, shape, axis) + window * (D - W)
    head = jnp.zeros(shape, jnp.int32)
    for h in range(1, VIEWS):
        head = head + jnp.where(feature >= h * HEAD, 1, 0)
    return feature, head


def masks(window):
    _, rows = heads_of((W, W), 0, window)
    _, cols = heads_of((W, W), 1, window)
    own = (rows < VIEWS // 2) if window == 0 else (rows >= VIEWS // 2)
    return (rows == cols) & own


def eye_of(size):
    return lax.broadcasted_iota(jnp.int32, (size, size), 0) == lax.broadcasted_iota(
        jnp.int32, (size, size), 1
    )


def to_col(eye, v):
    return jnp.sum(jnp.where(eye, v, 0.0), axis=1, keepdims=True)


def to_row(eye, v):
    return jnp.sum(jnp.where(eye, v, 0.0), axis=0, keepdims=True)


def sharp_col(sharp_ref, window):
    _, head = heads_of((W, 1), 0, window)
    sharp = jnp.zeros((W, 1), f32)
    for h in range(VIEWS):
        sharp = jnp.where(head == h, sharp_ref[h], sharp)
    return sharp


def rows_of(first, load, size):
    base = jnp.minimum(first // 8 * 8, size - PICK)
    block = load(pl.ds(pl.multiple_of(base, 8), PICK))
    return pltpu.roll(block, PICK - (first - base), 0)


scale = 1.0 / math.sqrt(262144)


def solve_kernel(
    place_ref, sharp_ref, w_ref, f_ref, m0, m1, m2, m3, o0, o1, o2, o3,
    gv_ref, m_ref, d_ref, rows_ref, block_ref, a_ref, b_ref, c_ref, t_ref, att_ref,
):
    core, first, chip = place_ref[0], place_ref[1], place_ref[2]
    for k, mine_ref, other_ref in zip((0,) + AWAY, (m0, m1, m2, m3), (o0, o1, o2, o3)):
        block_ref[core, chip ^ k] = mine_ref[...].reshape(2, T, T)
        block_ref[1 - core, chip ^ k] = other_ref[...].reshape(2, T, T)
    for at, (name, i, j) in enumerate(BLOCKS):
        block = block_ref[place_of(at)]
        ref = a_ref if name == "a" else b_ref
        ref[i * T : (i + 1) * T, j * T : (j + 1) * T] = block
        if name == "a" and i != j:
            ref[j * T : (j + 1) * T, i * T : (i + 1) * T] = block.T
    a_s, b_s = split(a_ref[...]), split(b_ref[...])
    ws, fs = split(w_ref[...]), split(f_ref[...])
    t = dot3(a_s, cut(ws, ALL, slice(0, 2 * D)), NN)
    t_ref[...] = t
    c = dot3(cut(ws, ALL, slice(2 * D, 3 * D)), b_s, TN)
    c_ref[...] = c
    c_s = split(c)
    square = jnp.sum(w_ref[:, : 2 * D] * t, axis=0, keepdims=True)
    inverse = lax.rsqrt(jnp.maximum(square, 0.0) + epsilon)
    q_inv, k_inv = inverse[:, :D], inverse[:, D:]
    tks = split(t[:, D:])
    t_rows = rows_of(first, lambda rows: t_ref[rows], D)
    b_rows = rows_of(first, lambda rows: b_ref[rows], D)
    tq_rows, tk_rows = split(t_rows[:, :D]), split(t_rows[:, D:])
    eye = eye_of(W)
    attentions, covs, mixers = [], [], []
    for window, span in enumerate(WINDOWS):
        same = masks(window)
        cov = dot3(cut(ws, ALL, span), cut(tks, ALL, span), TN)
        cov = jnp.where(same, cov * to_col(eye, q_inv[:, span]) * k_inv[:, span], 0.0)
        table = jnp.where(same, jnp.exp(sharp_col(sharp_ref, window) * cov), 0.0)
        total = jnp.sum(table, axis=1, keepdims=True)
        attention = table / jnp.where(total > 0.0, total, 1.0)
        att_ref[window] = attention
        attentions.append(attention)
        covs.append(cov)
        mixers.append(dot3(cut(fs, span, ALL), split(attention), TN))
    gv = split(join(mixers))
    gv_ref[0], gv_ref[1] = gv
    window = jnp.where(first >= D // 2, 1, 0)
    offset = pl.multiple_of(window * (D - W), T)
    att_rows = rows_of(first - offset, lambda rows: att_ref[window, rows], W)
    c_part = split(c_ref[pl.ds(offset, W)])
    rows_ref[:, 2 * D : 3 * D] = row_dot3(split(b_rows), gv, NN)[:8] * scale
    rows_ref[:, 3 * D : 4 * D] = row_dot3(split(att_rows), c_part, NN)[:8] * scale
    q_sum, k_sum, q_rows, k_rows = [], [], [], []
    temp = jnp.zeros((1, T), f32)
    for window, span in enumerate(WINDOWS):
        attention, cov = attentions[window], covs[window]
        sharp = sharp_col(sharp_ref, window)
        attention_grad = dot3(cut(fs, span, ALL), cut(c_s, span, ALL), NT)
        inner = jnp.sum(attention * attention_grad, axis=1, keepdims=True)
        score_grad = attention * (attention_grad - inner)
        weighed = score_grad * cov
        by_feature = jnp.sum(weighed, axis=1, keepdims=True)
        q_sum.append(to_row(eye, sharp * by_feature))
        k_sum.append(jnp.sum(sharp * weighed, axis=0, keepdims=True))
        m_s = split(sharp * score_grad * to_col(eye, q_inv[:, span]) * k_inv[:, span])
        m_ref[0, window], m_ref[1, window] = m_s
        q_rows.append(row_dot3(cut(tk_rows, ALL, span), m_s, NT))
        k_rows.append(row_dot3(cut(tq_rows, ALL, span), m_s, NN))
        _, head = heads_of((W, T), 0, window)
        lane = lax.broadcasted_iota(jnp.int32, (W, T), 1)
        temp += jnp.sum(jnp.where(head == lane, by_feature, 0.0), axis=0, keepdims=True)
    d_q = join(q_sum) * (q_inv * q_inv)
    d_k = join(k_sum) * (k_inv * k_inv)
    d_ref[0:1] = d_q
    d_ref[1:2] = d_k
    rows_ref[:, :D] = (join(q_rows) - t_rows[:, :D] * d_q)[:8] * scale
    rows_ref[:, D : 2 * D] = (join(k_rows) - t_rows[:, D:] * d_k)[:8] * scale
    rows_ref[:, 4 * D :] = jnp.broadcast_to(temp * scale, (8, T))


def output_kernel(
    x_ref, u_ref, w_ref, gv_ref, m_ref, d_ref, out_hbm, out_ref, sems
):
    ws = split(w_ref[...])
    q_parts, k_parts = [], []
    for window, span in enumerate(WINDOWS):
        m_s = (m_ref[0, window], m_ref[1, window])
        q_parts.append(dot3(cut(ws, ALL, slice(D + span.start, D + span.stop)), m_s, NT))
        k_parts.append(dot3(cut(ws, ALL, span), m_s, NN))
    gq = split(join(q_parts) - w_ref[:, :D] * d_ref[0:1])
    gk = split(join(k_parts) - w_ref[:, D : 2 * D] * d_ref[1:2])
    g = tuple(jnp.concatenate([one, two], axis=1) for one, two in zip(gq, gk))
    gv = (gv_ref[0], gv_ref[1])
    p = split(dot3(g, cut(ws, ALL, slice(0, 2 * D)), NT))
    r = split(dot3(gv, cut(ws, ALL, slice(2 * D, 3 * D)), NT))
    factors = tuple(jnp.concatenate([one, two], axis=0) for one, two in zip(p, r))
    tokens = x_ref.shape[0]
    step = tokens // 8
    copies = []
    for k in range(8):
        piece = pl.ds(k * step, step)
        xs, us = split(x_ref[piece]), split(u_ref[piece])
        token = tuple(jnp.concatenate([one, two], axis=1) for one, two in zip(xs, us))
        out_ref[piece] = dot3(token, factors, NN)
        copy = pltpu.make_async_copy(out_ref.at[piece], out_hbm.at[piece], sems.at[k])
        copy.start()
        copies.append(copy)
    for copy in copies:
        copy.wait()


def total_kernel(own_ref, two_ref, three_ref, one_ref, mixer_ref, output_ref, sharp_ref):
    total = (own_ref[...] + two_ref[...]) + (one_ref[...] + three_ref[...])
    mixer_ref[...] = total[:ROWS, : 3 * D]
    output_ref[...] = total[:ROWS, 3 * D : 4 * D]
    sharp_ref[...] = total[0:1, 4 * D : 4 * D + VIEWS]


smem = pl.BlockSpec(memory_space=pltpu.SMEM)
vmem = pl.BlockSpec(memory_space=pltpu.VMEM)
hbm = pl.BlockSpec(memory_space=pltpu.HBM)


def call(kernel, ins, outs, shapes, scratch=(), flops=0, limit=32):
    return pl.pallas_call(
        kernel,
        in_specs=ins,
        out_specs=outs,
        out_shape=[jax.ShapeDtypeStruct(*one) for one in shapes],
        scratch_shapes=list(scratch),
        compiler_params=pltpu.CompilerParams(vmem_limit_bytes=limit * 1024 * 1024),
        cost_estimate=pl.CostEstimate(flops=flops, bytes_accessed=4 * 1024 * 1024, transcendentals=0),
    )


def body(
    incoming_embeddings,
    stacked_projector,
    final_projector,
    sharpness_per_view,
    upstream_sensitivity,
):
    x = incoming_embeddings[0]
    u = upstream_sensitivity[0]
    tokens = x.shape[0]
    core, x_chip, z_chip = (lax.axis_index(axis) for axis in ("core", "x", "z"))
    ctx = (x_chip * Z_CHIPS + z_chip) * CORES + core
    chip = (x_chip ^ x_chip // 2) % 2 * 2 + z_chip % 2
    place = jnp.stack([core, ctx * ROWS, chip]).astype(jnp.int32)
    unit = 2 * 3 * D * D * D

    def in_hbm(array):
        return pltpu.with_memory_space_constraint(array, pltpu.HBM)

    half = ((HALF, T), f32)
    keep, send = call(
        gram_kernel,
        [smem, hbm, hbm],
        [vmem] * 2,
        [half] * 2,
        [
            pltpu.VMEM((tokens, D), f32),
            pltpu.VMEM((tokens, D), f32),
            pltpu.VMEM((CORES, SQUARE, 2, T, T), f32),
            pltpu.SemaphoreType.DMA((8,)),
        ],
        flops=6 * unit,
    )(place, in_hbm(x), in_hbm(u))

    def swap(array):
        return lax.ppermute(array, "core", [(0, 1), (1, 0)])

    def shift(array, axis, by):
        size = lax.axis_size(axis)
        return lax.ppermute(array, axis, [(i, (i + by) % size) for i in range(size)])

    def exchange(array, x_apart, z_apart):
        pairs = [
            (i * Z_CHIPS + j, (i ^ x_apart) * Z_CHIPS + (j ^ z_apart))
            for i in range(X_CHIPS)
            for j in range(Z_CHIPS)
        ]
        return lax.ppermute(array, ("x", "z"), pairs)

    def within_square(pieces):
        return [exchange(piece, k // 2, k % 2) for k, piece in zip(AWAY, pieces)]

    part = (keep + swap(send)).reshape(SQUARE, QUARTER, T)
    others = within_square([part[k] for k in AWAY])
    part = (part[0] + others[0]) + (others[1] + others[2])
    for apart in ((3, 0), (0, 6), (0, 2)):
        part = part + exchange(part, *apart)
    mine = [part] + within_square([part] * 3)
    other = [swap(piece) for piece in mine]

    gv, m, diagonal, rows = call(
        solve_kernel,
        [smem, smem] + [vmem] * 10,
        [vmem] * 4,
        [((2, D, D), bf16), ((2, 2, W, W), bf16), ((2, D), f32), ((8, 4 * D + T), f32)],
        [
            pltpu.VMEM((CORES, SQUARE, 2, T, T), f32),
            pltpu.VMEM((D, D), f32),
            pltpu.VMEM((D, D), f32),
            pltpu.VMEM((D, D), f32),
            pltpu.VMEM((D, 2 * D), f32),
            pltpu.VMEM((2, W, W), f32),
        ],
        flops=8 * unit,
    )(place, sharpness_per_view, stacked_projector, final_projector, *mine, *other)

    one, two, three = [shift(rows, "dp", k) for k in range(1, lax.axis_size("dp"))]
    (input_grad,) = call(
        output_kernel,
        [vmem] * 6,
        [hbm],
        [((tokens, D), f32)],
        [pltpu.VMEM((tokens, D), f32), pltpu.SemaphoreType.DMA((8,))],
        flops=12 * unit,
    )(x, u, stacked_projector, gv, m, diagonal)
    mixer_grad, output_grad, sharpness_grad = call(
        total_kernel,
        [vmem] * 4,
        [vmem] * 3,
        [((ROWS, 3 * D), f32), ((ROWS, D), f32), ((1, VIEWS), f32)],
    )(rows, two, three, one)
    return input_grad[None], mixer_grad, output_grad, sharpness_grad.reshape(VIEWS)


def solution(mesh):
    slides = mesh.shape["dp"]
    fine = Mesh(
        mesh.devices.reshape(slides, X_CHIPS, Z_CHIPS, CORES), ("dp", "x", "z", "core")
    )
    ctx = ("x", "z", "core")
    return jax.shard_map(
        body,
        mesh=fine,
        in_specs=(P("dp", ctx, None), P(), P(), P(), P("dp", ctx, None)),
        out_specs=(P("dp", ctx, None), P(ctx, None), P(ctx, None), P()),
        check_vma=False,
    )
```

```python
import functools
import math

import jax
import jax.numpy as jnp
from jax import lax
from jax.experimental import pallas as pl
from jax.experimental.pallas import tpu as pltpu
from jax.sharding import Mesh, PartitionSpec as P

epsilon = 1e-06
D = 384
VIEWS = 8
HEAD = D // VIEWS
T = 128
W = 256
X_CHIPS, Z_CHIPS, CORES = 4, 8, 2
SHARES = X_CHIPS * Z_CHIPS
ROWS = D // (SHARES * CORES)
HALF = 8 * T
SQUARE = 4
AWAY = (3, 2, 1)
QUARTER = HALF // SQUARE
PICK = 16
BLOCKS = [("a", i, j) for i in range(3) for j in range(i, 3)]
BLOCKS += [("b", i, j) for i in range(3) for j in range(3)]


def place_of(at):
    return at // 8, at % 8 // 2, at % 2


f32, bf16 = jnp.float32, jnp.bfloat16
NN = ((1,), (0,))
NT = ((1,), (1,))
TN = ((0,), (0,))


def split(a):
    high = a.astype(bf16)
    return high, (a - high.astype(f32)).astype(bf16)


def dot3(a, b, dims):
    (ca,), (cb,) = dims
    return lax.dot_general(
        jnp.concatenate([a[0], a[0], a[1]], axis=ca),
        jnp.concatenate([b[0], b[1], b[0]], axis=cb),
        (dims, ((), ())),
        preferred_element_type=f32,
    )


def row_dot3(a, b, dims):
    d = functools.partial(
        lax.dot_general, dimension_numbers=(dims, ((), ())), preferred_element_type=f32
    )
    both = d(jnp.concatenate(a, axis=0), b[0])
    return both[:PICK] + both[PICK:] + d(a[0], b[1])


def cut(pair, rows, cols):
    return pair[0][rows, cols], pair[1][rows, cols]


ALL = slice(None)
WINDOWS = (slice(0, W), slice(D - W, D))


def join(parts):
    one, two = parts
    return jnp.concatenate([one[:, :T], one[:, T:] + two[:, :T], two[:, T:]], axis=1)


def gram_kernel(place_ref, x_hbm, u_hbm, keep_ref, send_ref, x_ref, u_ref, pay_ref, sems):
    step = x_ref.shape[0] // 2
    copies = []
    for part in range(2):
        piece = pl.ds(part * step, step)
        for at, (source, target) in enumerate(((x_hbm, x_ref), (u_hbm, u_ref))):
            copy = pltpu.make_async_copy(
                source.at[piece], target.at[piece], sems.at[part * 2 + at]
            )
            copy.start()
            copies.append(copy)
    d = functools.partial(
        lax.dot_general, dimension_numbers=(TN, ((), ())), preferred_element_type=f32
    )
    sums = []
    for part in range(2):
        piece = pl.ds(part * step, step)
        copies[2 * part].wait()
        copies[2 * part + 1].wait()
        xh, xl = split(x_ref[piece])
        uh, ul = split(u_ref[piece])
        wide = d(xh, jnp.concatenate([xh, xl, uh, ul], axis=1))
        mixed = wide[:, 2 * D : 3 * D] + wide[:, 3 * D :] + d(xl, uh)
        sums.append((wide[:, :D], wide[:, D : 2 * D], mixed))
    whole, cross, mixed = (one + two for one, two in zip(*sums))
    grams = {"a": whole + cross + cross.T, "b": mixed}
    for at, (name, i, j) in enumerate(BLOCKS):
        pay_ref[place_of(at)] = grams[name][i * T : (i + 1) * T, j * T : (j + 1) * T]
    pay_ref[place_of(15)] = jnp.zeros((T, T), f32)
    core, chip = place_ref[0], place_ref[2]
    for k in range(SQUARE):
        to = chip ^ k
        piece = pl.ds(k * QUARTER, QUARTER)
        keep_ref[piece] = pay_ref[core, to].reshape(QUARTER, T)
        send_ref[piece] = pay_ref[1 - core, to].reshape(QUARTER, T)


def heads_of(shape, axis, window):
    feature = lax.broadcasted_iota(jnp.int32, shape, axis) + window * (D - W)
    head = jnp.zeros(shape, jnp.int32)
    for h in range(1, VIEWS):
        head = head + jnp.where(feature >= h * HEAD, 1, 0)
    return feature, head


def masks(window):
    _, rows = heads_of((W, W), 0, window)
    _, cols = heads_of((W, W), 1, window)
    own = (rows < VIEWS // 2) if window == 0 else (rows >= VIEWS // 2)
    return (rows == cols) & own


def eye_of(size):
    return lax.broadcasted_iota(jnp.int32, (size, size), 0) == lax.broadcasted_iota(
        jnp.int32, (size, size), 1
    )


def to_col(eye, v):
    return jnp.sum(jnp.where(eye, v, 0.0), axis=1, keepdims=True)


def to_row(eye, v):
    return jnp.sum(jnp.where(eye, v, 0.0), axis=0, keepdims=True)


def sharp_col(sharp_ref, window):
    _, head = heads_of((W, 1), 0, window)
    sharp = jnp.zeros((W, 1), f32)
    for h in range(VIEWS):
        sharp = jnp.where(head == h, sharp_ref[h], sharp)
    return sharp


def rows_of(first, load, size):
    base = jnp.minimum(first // 8 * 8, size - PICK)
    block = load(pl.ds(pl.multiple_of(base, 8), PICK))
    return pltpu.roll(block, PICK - (first - base), 0)


scale = 1.0 / math.sqrt(262144)


def solve_kernel(
    place_ref, sharp_ref, w_ref, f_ref, m0, m1, m2, m3, o0, o1, o2, o3,
    gv_ref, m_ref, d_ref, rows_ref, block_ref, a_ref, b_ref, c_ref, t_ref, att_ref,
):
    core, first, chip = place_ref[0], place_ref[1], place_ref[2]
    for k, mine_ref, other_ref in zip((0,) + AWAY, (m0, m1, m2, m3), (o0, o1, o2, o3)):
        block_ref[core, chip ^ k] = mine_ref[...].reshape(2, T, T)
        block_ref[1 - core, chip ^ k] = other_ref[...].reshape(2, T, T)
    for at, (name, i, j) in enumerate(BLOCKS):
        block = block_ref[place_of(at)]
        ref = a_ref if name == "a" else b_ref
        ref[i * T : (i + 1) * T, j * T : (j + 1) * T] = block
        if name == "a" and i != j:
            ref[j * T : (j + 1) * T, i * T : (i + 1) * T] = block.T
    a_s, b_s = split(a_ref[...]), split(b_ref[...])
    ws, fs = split(w_ref[...]), split(f_ref[...])
    tk = dot3(a_s, cut(ws, ALL, slice(D, 2 * D)), NN)
    c = dot3(cut(ws, ALL, slice(2 * D, 3 * D)), b_s, TN)
    tks, c_s = split(tk), split(c)
    raw = [dot3(cut(ws, ALL, span), cut(tks, ALL, span), TN) for span in WINDOWS]
    tq = dot3(a_s, cut(ws, ALL, slice(0, D)), NN)
    t_ref[:, :D], t_ref[:, D:] = tq, tk
    c_ref[...] = c
    attention_grads = [
        dot3(cut(fs, span, ALL), cut(c_s, span, ALL), NT) for span in WINDOWS
    ]
    q_square = jnp.sum(w_ref[:, :D] * tq, axis=0, keepdims=True)
    k_square = jnp.sum(w_ref[:, D : 2 * D] * tk, axis=0, keepdims=True)
    q_inv = lax.rsqrt(jnp.maximum(q_square, 0.0) + epsilon)
    k_inv = lax.rsqrt(jnp.maximum(k_square, 0.0) + epsilon)
    t_rows = rows_of(first, lambda rows: t_ref[rows], D)
    b_rows = rows_of(first, lambda rows: b_ref[rows], D)
    tq_rows, tk_rows = split(t_rows[:, :D]), split(t_rows[:, D:])
    eye = eye_of(W)
    attentions, covs, mixers = [], [], []
    for window, span in enumerate(WINDOWS):
        same = masks(window)
        cov = jnp.where(same, raw[window] * to_col(eye, q_inv[:, span]) * k_inv[:, span], 0.0)
        table = jnp.where(same, jnp.exp(sharp_col(sharp_ref, window) * cov), 0.0)
        total = jnp.sum(table, axis=1, keepdims=True)
        attention = table / jnp.where(total > 0.0, total, 1.0)
        att_ref[window] = attention
        attentions.append(attention)
        covs.append(cov)
        mixers.append(dot3(cut(fs, span, ALL), split(attention), TN))
    gv = split(join(mixers))
    gv_ref[0], gv_ref[1] = gv
    window = jnp.where(first >= D // 2, 1, 0)
    offset = pl.multiple_of(window * (D - W), T)
    att_rows = rows_of(first - offset, lambda rows: att_ref[window, rows], W)
    c_part = split(c_ref[pl.ds(offset, W)])
    rows_ref[:, 2 * D : 3 * D] = row_dot3(split(b_rows), gv, NN)[:8] * scale
    rows_ref[:, 3 * D : 4 * D] = row_dot3(split(att_rows), c_part, NN)[:8] * scale
    q_sum, k_sum, q_rows, k_rows = [], [], [], []
    temp = jnp.zeros((1, T), f32)
    for window, span in enumerate(WINDOWS):
        attention, cov = attentions[window], covs[window]
        sharp = sharp_col(sharp_ref, window)
        attention_grad = attention_grads[window]
        inner = jnp.sum(attention * attention_grad, axis=1, keepdims=True)
        score_grad = attention * (attention_grad - inner)
        weighed = score_grad * cov
        by_feature = jnp.sum(weighed, axis=1, keepdims=True)
        q_sum.append(to_row(eye, sharp * by_feature))
        k_sum.append(jnp.sum(sharp * weighed, axis=0, keepdims=True))
        m_s = split(sharp * score_grad * to_col(eye, q_inv[:, span]) * k_inv[:, span])
        m_ref[0, window], m_ref[1, window] = m_s
        q_rows.append(row_dot3(cut(tk_rows, ALL, span), m_s, NT))
        k_rows.append(row_dot3(cut(tq_rows, ALL, span), m_s, NN))
        _, head = heads_of((W, T), 0, window)
        lane = lax.broadcasted_iota(jnp.int32, (W, T), 1)
        temp += jnp.sum(jnp.where(head == lane, by_feature, 0.0), axis=0, keepdims=True)
    d_q = join(q_sum) * (q_inv * q_inv)
    d_k = join(k_sum) * (k_inv * k_inv)
    d_ref[0:1] = d_q
    d_ref[1:2] = d_k
    rows_ref[:, :D] = (join(q_rows) - t_rows[:, :D] * d_q)[:8] * scale
    rows_ref[:, D : 2 * D] = (join(k_rows) - t_rows[:, D:] * d_k)[:8] * scale
    rows_ref[:, 4 * D :] = jnp.broadcast_to(temp * scale, (8, T))


def output_kernel(
    x_ref, u_ref, w_ref, gv_ref, m_ref, d_ref, out_hbm, out_ref, sems
):
    ws = split(w_ref[...])
    q_parts, k_parts = [], []
    for window, span in enumerate(WINDOWS):
        m_s = (m_ref[0, window], m_ref[1, window])
        q_parts.append(dot3(cut(ws, ALL, slice(D + span.start, D + span.stop)), m_s, NT))
        k_parts.append(dot3(cut(ws, ALL, span), m_s, NN))
    gq = split(join(q_parts) - w_ref[:, :D] * d_ref[0:1])
    gk = split(join(k_parts) - w_ref[:, D : 2 * D] * d_ref[1:2])
    g = tuple(jnp.concatenate([one, two], axis=1) for one, two in zip(gq, gk))
    gv = (gv_ref[0], gv_ref[1])
    wqk = cut(ws, ALL, slice(0, 2 * D))
    corner = dot3(cut(g, slice(0, T), ALL), cut(wqk, slice(0, T), ALL), NT)
    others = dot3(g, cut(wqk, slice(T, D), ALL), NT)
    corner = jnp.concatenate([corner, others[:T, :T].T, others[:T, T:].T], axis=0)
    p = split(jnp.concatenate([corner, others], axis=1))
    r = split(dot3(gv, cut(ws, ALL, slice(2 * D, 3 * D)), NT))
    factors = tuple(jnp.concatenate([one, two], axis=0) for one, two in zip(p, r))
    tokens = x_ref.shape[0]
    step = tokens // 8
    copies = []
    for k in range(8):
        piece = pl.ds(k * step, step)
        xs, us = split(x_ref[piece]), split(u_ref[piece])
        token = tuple(jnp.concatenate([one, two], axis=1) for one, two in zip(xs, us))
        out_ref[piece] = dot3(token, factors, NN)
        copy = pltpu.make_async_copy(out_ref.at[piece], out_hbm.at[piece], sems.at[k])
        copy.start()
        copies.append(copy)
    for copy in copies:
        copy.wait()


def total_kernel(own_ref, two_ref, three_ref, one_ref, mixer_ref, output_ref, sharp_ref):
    total = (own_ref[...] + two_ref[...]) + (one_ref[...] + three_ref[...])
    mixer_ref[...] = total[:ROWS, : 3 * D]
    output_ref[...] = total[:ROWS, 3 * D : 4 * D]
    sharp_ref[...] = total[0:1, 4 * D : 4 * D + VIEWS]


smem = pl.BlockSpec(memory_space=pltpu.SMEM)
vmem = pl.BlockSpec(memory_space=pltpu.VMEM)
hbm = pl.BlockSpec(memory_space=pltpu.HBM)


def call(kernel, ins, outs, shapes, scratch=(), flops=0, limit=32):
    return pl.pallas_call(
        kernel,
        in_specs=ins,
        out_specs=outs,
        out_shape=[jax.ShapeDtypeStruct(*one) for one in shapes],
        scratch_shapes=list(scratch),
        compiler_params=pltpu.CompilerParams(vmem_limit_bytes=limit * 1024 * 1024),
        cost_estimate=pl.CostEstimate(flops=flops, bytes_accessed=4 * 1024 * 1024, transcendentals=0),
    )


def body(
    incoming_embeddings,
    stacked_projector,
    final_projector,
    sharpness_per_view,
    upstream_sensitivity,
):
    x = incoming_embeddings[0]
    u = upstream_sensitivity[0]
    tokens = x.shape[0]
    core, x_chip, z_chip = (lax.axis_index(axis) for axis in ("core", "x", "z"))
    ctx = (x_chip * Z_CHIPS + z_chip) * CORES + core
    chip = (x_chip ^ x_chip // 2) % 2 * 2 + z_chip % 2
    place = jnp.stack([core, ctx * ROWS, chip]).astype(jnp.int32)
    unit = 2 * 3 * D * D * D

    def in_hbm(array):
        return pltpu.with_memory_space_constraint(array, pltpu.HBM)

    half = ((HALF, T), f32)
    keep, send = call(
        gram_kernel,
        [smem, hbm, hbm],
        [vmem] * 2,
        [half] * 2,
        [
            pltpu.VMEM((tokens, D), f32),
            pltpu.VMEM((tokens, D), f32),
            pltpu.VMEM((CORES, SQUARE, 2, T, T), f32),
            pltpu.SemaphoreType.DMA((4,)),
        ],
        flops=6 * unit,
    )(place, in_hbm(x), in_hbm(u))

    def swap(array):
        return lax.ppermute(array, "core", [(0, 1), (1, 0)])

    def shift(array, axis, by):
        size = lax.axis_size(axis)
        return lax.ppermute(array, axis, [(i, (i + by) % size) for i in range(size)])

    def exchange(array, x_apart, z_apart):
        pairs = [
            (i * Z_CHIPS + j, (i ^ x_apart) * Z_CHIPS + (j ^ z_apart))
            for i in range(X_CHIPS)
            for j in range(Z_CHIPS)
        ]
        return lax.ppermute(array, ("x", "z"), pairs)

    def within_square(pieces):
        return [exchange(piece, k // 2, k % 2) for k, piece in zip(AWAY, pieces)]

    part = (keep + swap(send)).reshape(SQUARE, QUARTER, T)
    others = within_square([part[k] for k in AWAY])
    part = (part[0] + others[0]) + (others[1] + others[2])
    for apart in ((3, 0), (0, 6), (0, 2)):
        part = part + exchange(part, *apart)
    mine = [part] + within_square([part] * 3)
    other = [swap(piece) for piece in mine]

    gv, m, diagonal, rows = call(
        solve_kernel,
        [smem, smem] + [vmem] * 10,
        [vmem] * 4,
        [((2, D, D), bf16), ((2, 2, W, W), bf16), ((2, D), f32), ((8, 4 * D + T), f32)],
        [
            pltpu.VMEM((CORES, SQUARE, 2, T, T), f32),
            pltpu.VMEM((D, D), f32),
            pltpu.VMEM((D, D), f32),
            pltpu.VMEM((D, D), f32),
            pltpu.VMEM((D, 2 * D), f32),
            pltpu.VMEM((2, W, W), f32),
        ],
        flops=8 * unit,
    )(place, sharpness_per_view, stacked_projector, final_projector, *mine, *other)

    one, two, three = [shift(rows, "dp", k) for k in range(1, lax.axis_size("dp"))]
    (input_grad,) = call(
        output_kernel,
        [vmem] * 6,
        [hbm],
        [((tokens, D), f32)],
        [pltpu.VMEM((tokens, D), f32), pltpu.SemaphoreType.DMA((8,))],
        flops=12 * unit,
    )(x, u, stacked_projector, gv, m, diagonal)
    mixer_grad, output_grad, sharpness_grad = call(
        total_kernel,
        [vmem] * 4,
        [vmem] * 3,
        [((ROWS, 3 * D), f32), ((ROWS, D), f32), ((1, VIEWS), f32)],
    )(rows, two, three, one)
    return input_grad[None], mixer_grad, output_grad, sharpness_grad.reshape(VIEWS)


def solution(mesh):
    slides = mesh.shape["dp"]
    fine = Mesh(
        mesh.devices.reshape(slides, X_CHIPS, Z_CHIPS, CORES), ("dp", "x", "z", "core")
    )
    ctx = ("x", "z", "core")
    return jax.shard_map(
        body,
        mesh=fine,
        in_specs=(P("dp", ctx, None), P(), P(), P(), P("dp", ctx, None)),
        out_specs=(P("dp", ctx, None), P(ctx, None), P(ctx, None), P()),
        check_vma=False,
    )
```

```python
import functools
import math

import jax
import jax.numpy as jnp
from jax import lax
from jax.experimental import pallas as pl
from jax.experimental.pallas import tpu as pltpu
from jax.sharding import Mesh, PartitionSpec as P

epsilon = 1e-06
D = 384
VIEWS = 8
HEAD = D // VIEWS
T = 128
W = 256
X_CHIPS, Z_CHIPS, CORES = 4, 8, 2
SHARES = X_CHIPS * Z_CHIPS
ROWS = D // (SHARES * CORES)
HALF = 7 * T
SQUARE = 4
AWAY = (3, 2, 1)
QUARTER = HALF // SQUARE
PICK = 16
BLOCKS = [("a", 0, 1), ("a", 0, 2), ("a", 1, 2), ("pair", 0, 0), ("last", 0, 0)]
BLOCKS += [("b", i, j) for i in range(3) for j in range(3)]


def place_of(at):
    return at // 7, slice(at % 7 * T, (at % 7 + 1) * T)


def quarter_of(place):
    return pl.ds(pl.multiple_of(place * QUARTER, 8), QUARTER)


f32, bf16 = jnp.float32, jnp.bfloat16
NN = ((1,), (0,))
NT = ((1,), (1,))
TN = ((0,), (0,))


def split(a):
    high = a.astype(bf16)
    return high, (a - high.astype(f32)).astype(bf16)


def dot3(a, b, dims):
    (ca,), (cb,) = dims
    return lax.dot_general(
        jnp.concatenate([a[0], a[0], a[1]], axis=ca),
        jnp.concatenate([b[0], b[1], b[0]], axis=cb),
        (dims, ((), ())),
        preferred_element_type=f32,
    )


def row_dot3(a, b, dims):
    d = functools.partial(
        lax.dot_general, dimension_numbers=(dims, ((), ())), preferred_element_type=f32
    )
    both = d(jnp.concatenate(a, axis=0), b[0])
    return both[:PICK] + both[PICK:] + d(a[0], b[1])


def cut(pair, rows, cols):
    return pair[0][rows, cols], pair[1][rows, cols]


ALL = slice(None)
WINDOWS = (slice(0, W), slice(D - W, D))


def join(parts):
    one, two = parts
    return jnp.concatenate([one[:, :T], one[:, T:] + two[:, :T], two[:, T:]], axis=1)


def iotas():
    return (lax.broadcasted_iota(jnp.int32, (T, T), axis) for axis in range(2))


def gram_kernel(place_ref, x_hbm, u_hbm, keep_ref, send_ref, x_ref, u_ref, pay_ref, sems):
    step = x_ref.shape[0] // 2
    copies = []
    for part in range(2):
        piece = pl.ds(part * step, step)
        for at, (source, target) in enumerate(((x_hbm, x_ref), (u_hbm, u_ref))):
            copy = pltpu.make_async_copy(
                source.at[piece], target.at[piece], sems.at[part * 2 + at]
            )
            copy.start()
            copies.append(copy)
    d = functools.partial(
        lax.dot_general, dimension_numbers=(TN, ((), ())), preferred_element_type=f32
    )
    sums = []
    for part in range(2):
        piece = pl.ds(part * step, step)
        copies[2 * part].wait()
        copies[2 * part + 1].wait()
        xh, xl = split(x_ref[piece])
        uh, ul = split(u_ref[piece])
        wide = d(xh, jnp.concatenate([xh, xl, uh, ul], axis=1))
        mixed = wide[:, 2 * D : 3 * D] + wide[:, 3 * D :] + d(xl, uh)
        sums.append((wide[:, :D], wide[:, D : 2 * D], mixed))
    whole, cross, mixed = (one + two for one, two in zip(*sums))
    a = whole + cross + cross.T
    for at, (name, i, j) in enumerate(BLOCKS):
        if name in ("a", "b"):
            source = a if name == "a" else mixed
            pay_ref[place_of(at)] = source[i * T : (i + 1) * T, j * T : (j + 1) * T]
    row, col = iotas()
    first, second, third = (a[i * T : (i + 1) * T, i * T : (i + 1) * T] for i in range(3))
    diagonal = jnp.sum(jnp.where(row == col, second, 0.0), axis=0, keepdims=True)
    hidden = jnp.where(row == T - 1, diagonal, diagonal[:, T - 1 :])
    pay_ref[place_of(3)] = jnp.where(row <= col, first, second)
    pay_ref[place_of(4)] = jnp.where(row <= col, third, hidden)
    core, chip = place_ref[0], place_ref[2]
    for k in range(SQUARE):
        to = chip ^ k
        piece = pl.ds(k * QUARTER, QUARTER)
        keep_ref[piece] = pay_ref[core, quarter_of(to)]
        send_ref[piece] = pay_ref[1 - core, quarter_of(to)]


def heads_of(shape, axis, window):
    feature = lax.broadcasted_iota(jnp.int32, shape, axis) + window * (D - W)
    head = jnp.zeros(shape, jnp.int32)
    for h in range(1, VIEWS):
        head = head + jnp.where(feature >= h * HEAD, 1, 0)
    return feature, head


def masks(window):
    _, rows = heads_of((W, W), 0, window)
    _, cols = heads_of((W, W), 1, window)
    own = (rows < VIEWS // 2) if window == 0 else (rows >= VIEWS // 2)
    return (rows == cols) & own


def eye_of(size):
    return lax.broadcasted_iota(jnp.int32, (size, size), 0) == lax.broadcasted_iota(
        jnp.int32, (size, size), 1
    )


def to_col(eye, v):
    return jnp.sum(jnp.where(eye, v, 0.0), axis=1, keepdims=True)


def to_row(eye, v):
    return jnp.sum(jnp.where(eye, v, 0.0), axis=0, keepdims=True)


def sharp_col(sharp_ref, window):
    _, head = heads_of((W, 1), 0, window)
    sharp = jnp.zeros((W, 1), f32)
    for h in range(VIEWS):
        sharp = jnp.where(head == h, sharp_ref[h], sharp)
    return sharp


def rows_of(first, load, size):
    base = jnp.minimum(first // 8 * 8, size - PICK)
    block = load(pl.ds(pl.multiple_of(base, 8), PICK))
    return pltpu.roll(block, PICK - (first - base), 0)


scale = 1.0 / math.sqrt(262144)


def solve_kernel(
    place_ref, sharp_ref, w_ref, f_ref, m0, m1, m2, m3, o0, o1, o2, o3,
    gv_ref, m_ref, d_ref, rows_ref, block_ref, a_ref, b_ref, c_ref, t_ref, att_ref,
):
    core, first, chip = place_ref[0], place_ref[1], place_ref[2]
    for k, mine_ref, other_ref in zip((0,) + AWAY, (m0, m1, m2, m3), (o0, o1, o2, o3)):
        block_ref[core, quarter_of(chip ^ k)] = mine_ref[...]
        block_ref[1 - core, quarter_of(chip ^ k)] = other_ref[...]
    for at, (name, i, j) in enumerate(BLOCKS):
        if name in ("a", "b"):
            block = block_ref[place_of(at)]
            ref = a_ref if name == "a" else b_ref
            ref[i * T : (i + 1) * T, j * T : (j + 1) * T] = block
            if name == "a":
                ref[j * T : (j + 1) * T, i * T : (i + 1) * T] = block.T
    row, col = iotas()
    pair, last = block_ref[place_of(3)], block_ref[place_of(4)]
    pair_t = pair.T
    diagonal = jnp.where(col[:1] == T - 1, last[T // 2 : T // 2 + 1, :1], last[T - 1 :])
    a_ref[:T, :T] = jnp.where(row <= col, pair, pair_t)
    second = jnp.where(row > col, pair, pair_t)
    a_ref[T : 2 * T, T : 2 * T] = jnp.where(row == col, diagonal, second)
    a_ref[2 * T :, 2 * T :] = jnp.where(row <= col, last, last.T)
    a_s, b_s = split(a_ref[...]), split(b_ref[...])
    ws, fs = split(w_ref[...]), split(f_ref[...])
    tk = dot3(a_s, cut(ws, ALL, slice(D, 2 * D)), NN)
    c = dot3(cut(ws, ALL, slice(2 * D, 3 * D)), b_s, TN)
    tks, c_s = split(tk), split(c)
    raw = [dot3(cut(ws, ALL, span), cut(tks, ALL, span), TN) for span in WINDOWS]
    tq = dot3(a_s, cut(ws, ALL, slice(0, D)), NN)
    t_ref[:, :D], t_ref[:, D:] = tq, tk
    c_ref[...] = c
    attention_grads = [
        dot3(cut(fs, span, ALL), cut(c_s, span, ALL), NT) for span in WINDOWS
    ]
    q_square = jnp.sum(w_ref[:, :D] * tq, axis=0, keepdims=True)
    k_square = jnp.sum(w_ref[:, D : 2 * D] * tk, axis=0, keepdims=True)
    q_inv = lax.rsqrt(jnp.maximum(q_square, 0.0) + epsilon)
    k_inv = lax.rsqrt(jnp.maximum(k_square, 0.0) + epsilon)
    t_rows = rows_of(first, lambda rows: t_ref[rows], D)
    b_rows = rows_of(first, lambda rows: b_ref[rows], D)
    tq_rows, tk_rows = split(t_rows[:, :D]), split(t_rows[:, D:])
    eye = eye_of(W)
    attentions, covs, mixers = [], [], []
    for window, span in enumerate(WINDOWS):
        same = masks(window)
        cov = jnp.where(same, raw[window] * to_col(eye, q_inv[:, span]) * k_inv[:, span], 0.0)
        table = jnp.where(same, jnp.exp(sharp_col(sharp_ref, window) * cov), 0.0)
        total = jnp.sum(table, axis=1, keepdims=True)
        attention = table / jnp.where(total > 0.0, total, 1.0)
        att_ref[window] = attention
        attentions.append(attention)
        covs.append(cov)
        mixers.append(dot3(cut(fs, span, ALL), split(attention), TN))
    gv = split(join(mixers))
    gv_ref[0], gv_ref[1] = gv
    window = jnp.where(first >= D // 2, 1, 0)
    offset = pl.multiple_of(window * (D - W), T)
    att_rows = rows_of(first - offset, lambda rows: att_ref[window, rows], W)
    c_part = split(c_ref[pl.ds(offset, W)])
    rows_ref[:, 2 * D : 3 * D] = row_dot3(split(b_rows), gv, NN)[:8] * scale
    rows_ref[:, 3 * D : 4 * D] = row_dot3(split(att_rows), c_part, NN)[:8] * scale
    q_sum, k_sum, q_rows, k_rows = [], [], [], []
    temp = jnp.zeros((1, T), f32)
    for window, span in enumerate(WINDOWS):
        attention, cov = attentions[window], covs[window]
        sharp = sharp_col(sharp_ref, window)
        attention_grad = attention_grads[window]
        inner = jnp.sum(attention * attention_grad, axis=1, keepdims=True)
        score_grad = attention * (attention_grad - inner)
        weighed = score_grad * cov
        by_feature = jnp.sum(weighed, axis=1, keepdims=True)
        q_sum.append(to_row(eye, sharp * by_feature))
        k_sum.append(jnp.sum(sharp * weighed, axis=0, keepdims=True))
        m_s = split(sharp * score_grad * to_col(eye, q_inv[:, span]) * k_inv[:, span])
        m_ref[0, window], m_ref[1, window] = m_s
        q_rows.append(row_dot3(cut(tk_rows, ALL, span), m_s, NT))
        k_rows.append(row_dot3(cut(tq_rows, ALL, span), m_s, NN))
        _, head = heads_of((W, T), 0, window)
        lane = lax.broadcasted_iota(jnp.int32, (W, T), 1)
        temp += jnp.sum(jnp.where(head == lane, by_feature, 0.0), axis=0, keepdims=True)
    d_q = join(q_sum) * (q_inv * q_inv)
    d_k = join(k_sum) * (k_inv * k_inv)
    d_ref[0:1] = d_q
    d_ref[1:2] = d_k
    rows_ref[:, :D] = (join(q_rows) - t_rows[:, :D] * d_q)[:8] * scale
    rows_ref[:, D : 2 * D] = (join(k_rows) - t_rows[:, D:] * d_k)[:8] * scale
    rows_ref[:, 4 * D :] = jnp.broadcast_to(temp * scale, (8, T))


def output_kernel(
    x_ref, u_ref, w_ref, gv_ref, m_ref, d_ref, out_hbm, out_ref, sems
):
    ws = split(w_ref[...])
    q_parts, k_parts = [], []
    for window, span in enumerate(WINDOWS):
        m_s = (m_ref[0, window], m_ref[1, window])
        q_parts.append(dot3(cut(ws, ALL, slice(D + span.start, D + span.stop)), m_s, NT))
        k_parts.append(dot3(cut(ws, ALL, span), m_s, NN))
    gq = split(join(q_parts) - w_ref[:, :D] * d_ref[0:1])
    gk = split(join(k_parts) - w_ref[:, D : 2 * D] * d_ref[1:2])
    g = tuple(jnp.concatenate([one, two], axis=1) for one, two in zip(gq, gk))
    gv = (gv_ref[0], gv_ref[1])
    wqk = cut(ws, ALL, slice(0, 2 * D))
    corner = dot3(cut(g, slice(0, T), ALL), cut(wqk, slice(0, T), ALL), NT)
    others = dot3(g, cut(wqk, slice(T, D), ALL), NT)
    corner = jnp.concatenate([corner, others[:T, :T].T, others[:T, T:].T], axis=0)
    p = split(jnp.concatenate([corner, others], axis=1))
    r = split(dot3(gv, cut(ws, ALL, slice(2 * D, 3 * D)), NT))
    factors = tuple(jnp.concatenate([one, two], axis=0) for one, two in zip(p, r))
    tokens = x_ref.shape[0]
    step = tokens // 8
    copies = []
    for k in range(8):
        piece = pl.ds(k * step, step)
        xs, us = split(x_ref[piece]), split(u_ref[piece])
        token = tuple(jnp.concatenate([one, two], axis=1) for one, two in zip(xs, us))
        out_ref[piece] = dot3(token, factors, NN)
        copy = pltpu.make_async_copy(out_ref.at[piece], out_hbm.at[piece], sems.at[k])
        copy.start()
        copies.append(copy)
    for copy in copies:
        copy.wait()


def total_kernel(own_ref, two_ref, three_ref, one_ref, mixer_ref, output_ref, sharp_ref):
    total = (own_ref[...] + two_ref[...]) + (one_ref[...] + three_ref[...])
    mixer_ref[...] = total[:ROWS, : 3 * D]
    output_ref[...] = total[:ROWS, 3 * D : 4 * D]
    sharp_ref[...] = total[0:1, 4 * D : 4 * D + VIEWS]


smem = pl.BlockSpec(memory_space=pltpu.SMEM)
vmem = pl.BlockSpec(memory_space=pltpu.VMEM)
hbm = pl.BlockSpec(memory_space=pltpu.HBM)


def call(kernel, ins, outs, shapes, scratch=(), flops=0, limit=32):
    return pl.pallas_call(
        kernel,
        in_specs=ins,
        out_specs=outs,
        out_shape=[jax.ShapeDtypeStruct(*one) for one in shapes],
        scratch_shapes=list(scratch),
        compiler_params=pltpu.CompilerParams(vmem_limit_bytes=limit * 1024 * 1024),
        cost_estimate=pl.CostEstimate(flops=flops, bytes_accessed=4 * 1024 * 1024, transcendentals=0),
    )


def body(
    incoming_embeddings,
    stacked_projector,
    final_projector,
    sharpness_per_view,
    upstream_sensitivity,
):
    x = incoming_embeddings[0]
    u = upstream_sensitivity[0]
    tokens = x.shape[0]
    core, x_chip, z_chip = (lax.axis_index(axis) for axis in ("core", "x", "z"))
    ctx = (x_chip * Z_CHIPS + z_chip) * CORES + core
    chip = (x_chip ^ x_chip // 2) % 2 * 2 + z_chip % 2
    place = jnp.stack([core, ctx * ROWS, chip]).astype(jnp.int32)
    unit = 2 * 3 * D * D * D

    def in_hbm(array):
        return pltpu.with_memory_space_constraint(array, pltpu.HBM)

    half = ((HALF, T), f32)
    keep, send = call(
        gram_kernel,
        [smem, hbm, hbm],
        [vmem] * 2,
        [half] * 2,
        [
            pltpu.VMEM((tokens, D), f32),
            pltpu.VMEM((tokens, D), f32),
            pltpu.VMEM((CORES, HALF, T), f32),
            pltpu.SemaphoreType.DMA((4,)),
        ],
        flops=6 * unit,
    )(place, in_hbm(x), in_hbm(u))

    def swap(array):
        return lax.ppermute(array, "core", [(0, 1), (1, 0)])

    def shift(array, axis, by):
        size = lax.axis_size(axis)
        return lax.ppermute(array, axis, [(i, (i + by) % size) for i in range(size)])

    def exchange(array, x_apart, z_apart):
        pairs = [
            (i * Z_CHIPS + j, (i ^ x_apart) * Z_CHIPS + (j ^ z_apart))
            for i in range(X_CHIPS)
            for j in range(Z_CHIPS)
        ]
        return lax.ppermute(array, ("x", "z"), pairs)

    def within_square(pieces):
        return [exchange(piece, k // 2, k % 2) for k, piece in zip(AWAY, pieces)]

    part = (keep + swap(send)).reshape(SQUARE, QUARTER, T)
    others = within_square([part[k] for k in AWAY])
    part = (part[0] + others[0]) + (others[1] + others[2])
    for apart in ((3, 0), (0, 6), (0, 2)):
        part = part + exchange(part, *apart)
    mine = [part] + within_square([part] * 3)
    other = [swap(piece) for piece in mine]

    gv, m, diagonal, rows = call(
        solve_kernel,
        [smem, smem] + [vmem] * 10,
        [vmem] * 4,
        [((2, D, D), bf16), ((2, 2, W, W), bf16), ((2, D), f32), ((8, 4 * D + T), f32)],
        [
            pltpu.VMEM((CORES, HALF, T), f32),
            pltpu.VMEM((D, D), f32),
            pltpu.VMEM((D, D), f32),
            pltpu.VMEM((D, D), f32),
            pltpu.VMEM((D, 2 * D), f32),
            pltpu.VMEM((2, W, W), f32),
        ],
        flops=8 * unit,
    )(place, sharpness_per_view, stacked_projector, final_projector, *mine, *other)

    one, two, three = [shift(rows, "dp", k) for k in range(1, lax.axis_size("dp"))]
    (input_grad,) = call(
        output_kernel,
        [vmem] * 6,
        [hbm],
        [((tokens, D), f32)],
        [pltpu.VMEM((tokens, D), f32), pltpu.SemaphoreType.DMA((8,))],
        flops=12 * unit,
    )(x, u, stacked_projector, gv, m, diagonal)
    mixer_grad, output_grad, sharpness_grad = call(
        total_kernel,
        [vmem] * 4,
        [vmem] * 3,
        [((ROWS, 3 * D), f32), ((ROWS, D), f32), ((1, VIEWS), f32)],
    )(rows, two, three, one)
    return input_grad[None], mixer_grad, output_grad, sharpness_grad.reshape(VIEWS)


def solution(mesh):
    slides = mesh.shape["dp"]
    fine = Mesh(
        mesh.devices.reshape(slides, X_CHIPS, Z_CHIPS, CORES), ("dp", "x", "z", "core")
    )
    ctx = ("x", "z", "core")
    return jax.shard_map(
        body,
        mesh=fine,
        in_specs=(P("dp", ctx, None), P(), P(), P(), P("dp", ctx, None)),
        out_specs=(P("dp", ctx, None), P(ctx, None), P(ctx, None), P()),
        check_vma=False,
    )
```

```python
import functools
import math

import jax
import jax.numpy as jnp
from jax import lax
from jax.experimental import pallas as pl
from jax.experimental.pallas import tpu as pltpu
from jax.sharding import Mesh, PartitionSpec as P

epsilon = 1e-06
D = 384
VIEWS = 8
HEAD = D // VIEWS
T = 128
W = 256
X_CHIPS, Z_CHIPS, CORES = 4, 8, 2
SHARES = X_CHIPS * Z_CHIPS
ROWS = D // (SHARES * CORES)
HALF = 7 * T
SQUARE = 4
AWAY = (3, 2, 1)
QUARTER = HALF // SQUARE
PICK = 16
BLOCKS = [("a", 0, 1), ("a", 0, 2), ("a", 1, 2), ("pair", 0, 0), ("last", 0, 0)]
BLOCKS += [("b", i, j) for i in range(3) for j in range(3)]


def place_of(at):
    return at // 7, slice(at % 7 * T, (at % 7 + 1) * T)


def quarter_of(place):
    return pl.ds(pl.multiple_of(place * QUARTER, 8), QUARTER)


f32, bf16 = jnp.float32, jnp.bfloat16
NN = ((1,), (0,))
NT = ((1,), (1,))
TN = ((0,), (0,))


def split(a):
    high = a.astype(bf16)
    return high, (a - high.astype(f32)).astype(bf16)


def dot3(a, b, dims):
    (ca,), (cb,) = dims
    return lax.dot_general(
        jnp.concatenate([a[0], a[0], a[1]], axis=ca),
        jnp.concatenate([b[0], b[1], b[0]], axis=cb),
        (dims, ((), ())),
        preferred_element_type=f32,
    )


def row_dot3(a, b, dims):
    d = functools.partial(
        lax.dot_general, dimension_numbers=(dims, ((), ())), preferred_element_type=f32
    )
    both = d(jnp.concatenate(a, axis=0), b[0])
    return both[:PICK] + both[PICK:] + d(a[0], b[1])


def cut(pair, rows, cols):
    return pair[0][rows, cols], pair[1][rows, cols]


ALL = slice(None)
WINDOWS = (slice(0, W), slice(D - W, D))


def join(parts):
    one, two = parts
    return jnp.concatenate([one[:, :T], one[:, T:] + two[:, :T], two[:, T:]], axis=1)


def iotas():
    return (lax.broadcasted_iota(jnp.int32, (T, T), axis) for axis in range(2))


def gram_kernel(place_ref, x_hbm, u_hbm, *refs):
    keeps, sends, (x_ref, u_ref, pay_ref, sems) = refs[:SQUARE], refs[SQUARE : 2 * SQUARE], refs[2 * SQUARE :]
    step = x_ref.shape[0] // 2
    copies = []
    for part in range(2):
        piece = pl.ds(part * step, step)
        for at, (source, target) in enumerate(((x_hbm, x_ref), (u_hbm, u_ref))):
            copy = pltpu.make_async_copy(
                source.at[piece], target.at[piece], sems.at[part * 2 + at]
            )
            copy.start()
            copies.append(copy)
    d = functools.partial(
        lax.dot_general, dimension_numbers=(TN, ((), ())), preferred_element_type=f32
    )
    sums = []
    for part in range(2):
        piece = pl.ds(part * step, step)
        copies[2 * part].wait()
        copies[2 * part + 1].wait()
        xh, xl = split(x_ref[piece])
        uh, ul = split(u_ref[piece])
        wide = d(xh, jnp.concatenate([xh, xl, uh, ul], axis=1))
        mixed = wide[:, 2 * D : 3 * D] + wide[:, 3 * D :] + d(xl, uh)
        sums.append((wide[:, :D], wide[:, D : 2 * D], mixed))
    whole, cross, mixed = (one + two for one, two in zip(*sums))
    a = whole + cross + cross.T
    for at, (name, i, j) in enumerate(BLOCKS):
        if name in ("a", "b"):
            source = a if name == "a" else mixed
            pay_ref[place_of(at)] = source[i * T : (i + 1) * T, j * T : (j + 1) * T]
    row, col = iotas()
    first, second, third = (a[i * T : (i + 1) * T, i * T : (i + 1) * T] for i in range(3))
    diagonal = jnp.sum(jnp.where(row == col, second, 0.0), axis=0, keepdims=True)
    hidden = jnp.where(row == T - 1, diagonal, diagonal[:, T - 1 :])
    pay_ref[place_of(3)] = jnp.where(row <= col, first, second)
    pay_ref[place_of(4)] = jnp.where(row <= col, third, hidden)
    core, chip = place_ref[0], place_ref[2]
    for k in range(SQUARE):
        to = chip ^ k
        keeps[k][...] = pay_ref[core, quarter_of(to)]
        sends[k][...] = pay_ref[1 - core, quarter_of(to)]


def heads_of(shape, axis, window):
    feature = lax.broadcasted_iota(jnp.int32, shape, axis) + window * (D - W)
    head = jnp.zeros(shape, jnp.int32)
    for h in range(1, VIEWS):
        head = head + jnp.where(feature >= h * HEAD, 1, 0)
    return feature, head


def masks(window):
    _, rows = heads_of((W, W), 0, window)
    _, cols = heads_of((W, W), 1, window)
    own = (rows < VIEWS // 2) if window == 0 else (rows >= VIEWS // 2)
    return (rows == cols) & own


def eye_of(size):
    return lax.broadcasted_iota(jnp.int32, (size, size), 0) == lax.broadcasted_iota(
        jnp.int32, (size, size), 1
    )


def to_col(eye, v):
    return jnp.sum(jnp.where(eye, v, 0.0), axis=1, keepdims=True)


def to_row(eye, v):
    return jnp.sum(jnp.where(eye, v, 0.0), axis=0, keepdims=True)


def sharp_col(sharp_ref, window):
    _, head = heads_of((W, 1), 0, window)
    sharp = jnp.zeros((W, 1), f32)
    for h in range(VIEWS):
        sharp = jnp.where(head == h, sharp_ref[h], sharp)
    return sharp


def rows_of(first, load, size):
    base = jnp.minimum(first // 8 * 8, size - PICK)
    block = load(pl.ds(pl.multiple_of(base, 8), PICK))
    return pltpu.roll(block, PICK - (first - base), 0)


scale = 1.0 / math.sqrt(262144)


def solve_kernel(
    place_ref, sharp_ref, w_ref, f_ref, m0, m1, m2, m3, o0, o1, o2, o3,
    gv_ref, m_ref, d_ref, rows_ref, block_ref, a_ref, b_ref, c_ref, t_ref, att_ref,
):
    core, first, chip = place_ref[0], place_ref[1], place_ref[2]
    for k, mine_ref, other_ref in zip((0,) + AWAY, (m0, m1, m2, m3), (o0, o1, o2, o3)):
        block_ref[core, quarter_of(chip ^ k)] = mine_ref[...]
        block_ref[1 - core, quarter_of(chip ^ k)] = other_ref[...]
    for at, (name, i, j) in enumerate(BLOCKS):
        if name in ("a", "b"):
            block = block_ref[place_of(at)]
            ref = a_ref if name == "a" else b_ref
            ref[i * T : (i + 1) * T, j * T : (j + 1) * T] = block
            if name == "a":
                ref[j * T : (j + 1) * T, i * T : (i + 1) * T] = block.T
    row, col = iotas()
    pair, last = block_ref[place_of(3)], block_ref[place_of(4)]
    pair_t = pair.T
    diagonal = jnp.where(col[:1] == T - 1, last[T // 2 : T // 2 + 1, :1], last[T - 1 :])
    a_ref[:T, :T] = jnp.where(row <= col, pair, pair_t)
    second = jnp.where(row > col, pair, pair_t)
    a_ref[T : 2 * T, T : 2 * T] = jnp.where(row == col, diagonal, second)
    a_ref[2 * T :, 2 * T :] = jnp.where(row <= col, last, last.T)
    a_s, b_s = split(a_ref[...]), split(b_ref[...])
    ws, fs = split(w_ref[...]), split(f_ref[...])
    tk = dot3(a_s, cut(ws, ALL, slice(D, 2 * D)), NN)
    c = dot3(cut(ws, ALL, slice(2 * D, 3 * D)), b_s, TN)
    tks, c_s = split(tk), split(c)
    raw = [dot3(cut(ws, ALL, span), cut(tks, ALL, span), TN) for span in WINDOWS]
    tq = dot3(a_s, cut(ws, ALL, slice(0, D)), NN)
    t_ref[:, :D], t_ref[:, D:] = tq, tk
    c_ref[...] = c
    attention_grads = [
        dot3(cut(fs, span, ALL), cut(c_s, span, ALL), NT) for span in WINDOWS
    ]
    q_square = jnp.sum(w_ref[:, :D] * tq, axis=0, keepdims=True)
    k_square = jnp.sum(w_ref[:, D : 2 * D] * tk, axis=0, keepdims=True)
    q_inv = lax.rsqrt(jnp.maximum(q_square, 0.0) + epsilon)
    k_inv = lax.rsqrt(jnp.maximum(k_square, 0.0) + epsilon)
    t_rows = rows_of(first, lambda rows: t_ref[rows], D)
    b_rows = rows_of(first, lambda rows: b_ref[rows], D)
    tq_rows, tk_rows = split(t_rows[:, :D]), split(t_rows[:, D:])
    eye = eye_of(W)
    attentions, covs, mixers = [], [], []
    for window, span in enumerate(WINDOWS):
        same = masks(window)
        cov = jnp.where(same, raw[window] * to_col(eye, q_inv[:, span]) * k_inv[:, span], 0.0)
        table = jnp.where(same, jnp.exp(sharp_col(sharp_ref, window) * cov), 0.0)
        total = jnp.sum(table, axis=1, keepdims=True)
        attention = table / jnp.where(total > 0.0, total, 1.0)
        att_ref[window] = attention
        attentions.append(attention)
        covs.append(cov)
        mixers.append(dot3(cut(fs, span, ALL), split(attention), TN))
    gv = split(join(mixers))
    gv_ref[0], gv_ref[1] = gv
    window = jnp.where(first >= D // 2, 1, 0)
    offset = pl.multiple_of(window * (D - W), T)
    att_rows = rows_of(first - offset, lambda rows: att_ref[window, rows], W)
    c_part = split(c_ref[pl.ds(offset, W)])
    rows_ref[:, 2 * D : 3 * D] = row_dot3(split(b_rows), gv, NN)[:8] * scale
    rows_ref[:, 3 * D : 4 * D] = row_dot3(split(att_rows), c_part, NN)[:8] * scale
    q_sum, k_sum, q_rows, k_rows = [], [], [], []
    temp = jnp.zeros((1, T), f32)
    for window, span in enumerate(WINDOWS):
        attention, cov = attentions[window], covs[window]
        sharp = sharp_col(sharp_ref, window)
        attention_grad = attention_grads[window]
        inner = jnp.sum(attention * attention_grad, axis=1, keepdims=True)
        score_grad = attention * (attention_grad - inner)
        weighed = score_grad * cov
        by_feature = jnp.sum(weighed, axis=1, keepdims=True)
        q_sum.append(to_row(eye, sharp * by_feature))
        k_sum.append(jnp.sum(sharp * weighed, axis=0, keepdims=True))
        m_s = split(sharp * score_grad * to_col(eye, q_inv[:, span]) * k_inv[:, span])
        m_ref[0, window], m_ref[1, window] = m_s
        q_rows.append(row_dot3(cut(tk_rows, ALL, span), m_s, NT))
        k_rows.append(row_dot3(cut(tq_rows, ALL, span), m_s, NN))
        _, head = heads_of((W, T), 0, window)
        lane = lax.broadcasted_iota(jnp.int32, (W, T), 1)
        temp += jnp.sum(jnp.where(head == lane, by_feature, 0.0), axis=0, keepdims=True)
    d_q = join(q_sum) * (q_inv * q_inv)
    d_k = join(k_sum) * (k_inv * k_inv)
    d_ref[0:1] = d_q
    d_ref[1:2] = d_k
    rows_ref[:, :D] = (join(q_rows) - t_rows[:, :D] * d_q)[:8] * scale
    rows_ref[:, D : 2 * D] = (join(k_rows) - t_rows[:, D:] * d_k)[:8] * scale
    rows_ref[:, 4 * D :] = jnp.broadcast_to(temp * scale, (8, T))


def output_kernel(
    x_ref, u_ref, w_ref, gv_ref, m_ref, d_ref, out_hbm, out_ref, sems
):
    ws = split(w_ref[...])
    q_parts, k_parts = [], []
    for window, span in enumerate(WINDOWS):
        m_s = (m_ref[0, window], m_ref[1, window])
        q_parts.append(dot3(cut(ws, ALL, slice(D + span.start, D + span.stop)), m_s, NT))
        k_parts.append(dot3(cut(ws, ALL, span), m_s, NN))
    gq = split(join(q_parts) - w_ref[:, :D] * d_ref[0:1])
    gk = split(join(k_parts) - w_ref[:, D : 2 * D] * d_ref[1:2])
    g = tuple(jnp.concatenate([one, two], axis=1) for one, two in zip(gq, gk))
    gv = (gv_ref[0], gv_ref[1])
    wqk = cut(ws, ALL, slice(0, 2 * D))
    corner = dot3(cut(g, slice(0, T), ALL), cut(wqk, slice(0, T), ALL), NT)
    others = dot3(g, cut(wqk, slice(T, D), ALL), NT)
    corner = jnp.concatenate([corner, others[:T, :T].T, others[:T, T:].T], axis=0)
    p = split(jnp.concatenate([corner, others], axis=1))
    r = split(dot3(gv, cut(ws, ALL, slice(2 * D, 3 * D)), NT))
    factors = tuple(jnp.concatenate([one, two], axis=0) for one, two in zip(p, r))
    tokens = x_ref.shape[0]
    step = tokens // 8
    copies = []
    for k in range(8):
        piece = pl.ds(k * step, step)
        xs, us = split(x_ref[piece]), split(u_ref[piece])
        token = tuple(jnp.concatenate([one, two], axis=1) for one, two in zip(xs, us))
        out_ref[piece] = dot3(token, factors, NN)
        copy = pltpu.make_async_copy(out_ref.at[piece], out_hbm.at[piece], sems.at[k])
        copy.start()
        copies.append(copy)
    for copy in copies:
        copy.wait()


def total_kernel(own_ref, two_ref, three_ref, one_ref, mixer_ref, output_ref, sharp_ref):
    total = (own_ref[...] + two_ref[...]) + (one_ref[...] + three_ref[...])
    mixer_ref[...] = total[:ROWS, : 3 * D]
    output_ref[...] = total[:ROWS, 3 * D : 4 * D]
    sharp_ref[...] = total[0:1, 4 * D : 4 * D + VIEWS]


smem = pl.BlockSpec(memory_space=pltpu.SMEM)
vmem = pl.BlockSpec(memory_space=pltpu.VMEM)
hbm = pl.BlockSpec(memory_space=pltpu.HBM)


def call(kernel, ins, outs, shapes, scratch=(), flops=0, limit=32):
    return pl.pallas_call(
        kernel,
        in_specs=ins,
        out_specs=outs,
        out_shape=[jax.ShapeDtypeStruct(*one) for one in shapes],
        scratch_shapes=list(scratch),
        compiler_params=pltpu.CompilerParams(vmem_limit_bytes=limit * 1024 * 1024),
        cost_estimate=pl.CostEstimate(flops=flops, bytes_accessed=4 * 1024 * 1024, transcendentals=0),
    )


def body(
    incoming_embeddings,
    stacked_projector,
    final_projector,
    sharpness_per_view,
    upstream_sensitivity,
):
    x = incoming_embeddings[0]
    u = upstream_sensitivity[0]
    tokens = x.shape[0]
    core, x_chip, z_chip = (lax.axis_index(axis) for axis in ("core", "x", "z"))
    ctx = (x_chip * Z_CHIPS + z_chip) * CORES + core
    chip = (x_chip ^ x_chip // 2) % 2 * 2 + z_chip % 2
    place = jnp.stack([core, ctx * ROWS, chip]).astype(jnp.int32)
    unit = 2 * 3 * D * D * D

    def in_hbm(array):
        return pltpu.with_memory_space_constraint(array, pltpu.HBM)

    quarter = ((QUARTER, T), f32)
    pieces = call(
        gram_kernel,
        [smem, hbm, hbm],
        [vmem] * 2 * SQUARE,
        [quarter] * 2 * SQUARE,
        [
            pltpu.VMEM((tokens, D), f32),
            pltpu.VMEM((tokens, D), f32),
            pltpu.VMEM((CORES, HALF, T), f32),
            pltpu.SemaphoreType.DMA((4,)),
        ],
        flops=6 * unit,
    )(place, in_hbm(x), in_hbm(u))

    def swap(array):
        return lax.ppermute(array, "core", [(0, 1), (1, 0)])

    def shift(array, axis, by):
        size = lax.axis_size(axis)
        return lax.ppermute(array, axis, [(i, (i + by) % size) for i in range(size)])

    def exchange(array, x_apart, z_apart):
        pairs = [
            (i * Z_CHIPS + j, (i ^ x_apart) * Z_CHIPS + (j ^ z_apart))
            for i in range(X_CHIPS)
            for j in range(Z_CHIPS)
        ]
        return lax.ppermute(array, ("x", "z"), pairs)

    def within_square(pieces):
        return [exchange(piece, k // 2, k % 2) for k, piece in zip(AWAY, pieces)]

    part = [keep + swap(send) for keep, send in zip(pieces[:SQUARE], pieces[SQUARE:])]
    others = [exchange(part[k], k // 2, k % 2) for k in reversed(AWAY)]
    part = (part[0] + others[0]) + (others[1] + others[2])
    for apart in ((3, 0), (0, 6), (0, 2)):
        part = part + exchange(part, *apart)
    mine = [part] + within_square([part] * 3)
    other = [swap(piece) for piece in mine]

    gv, m, diagonal, rows = call(
        solve_kernel,
        [smem, smem] + [vmem] * 10,
        [vmem] * 4,
        [((2, D, D), bf16), ((2, 2, W, W), bf16), ((2, D), f32), ((8, 4 * D + T), f32)],
        [
            pltpu.VMEM((CORES, HALF, T), f32),
            pltpu.VMEM((D, D), f32),
            pltpu.VMEM((D, D), f32),
            pltpu.VMEM((D, D), f32),
            pltpu.VMEM((D, 2 * D), f32),
            pltpu.VMEM((2, W, W), f32),
        ],
        flops=8 * unit,
    )(place, sharpness_per_view, stacked_projector, final_projector, *mine, *other)

    one, two, three = [shift(rows, "dp", k) for k in range(1, lax.axis_size("dp"))]
    (input_grad,) = call(
        output_kernel,
        [vmem] * 6,
        [hbm],
        [((tokens, D), f32)],
        [pltpu.VMEM((tokens, D), f32), pltpu.SemaphoreType.DMA((8,))],
        flops=12 * unit,
    )(x, u, stacked_projector, gv, m, diagonal)
    mixer_grad, output_grad, sharpness_grad = call(
        total_kernel,
        [vmem] * 4,
        [vmem] * 3,
        [((ROWS, 3 * D), f32), ((ROWS, D), f32), ((1, VIEWS), f32)],
    )(rows, two, three, one)
    return input_grad[None], mixer_grad, output_grad, sharpness_grad.reshape(VIEWS)


def solution(mesh):
    slides = mesh.shape["dp"]
    fine = Mesh(
        mesh.devices.reshape(slides, X_CHIPS, Z_CHIPS, CORES), ("dp", "x", "z", "core")
    )
    ctx = ("x", "z", "core")
    return jax.shard_map(
        body,
        mesh=fine,
        in_specs=(P("dp", ctx, None), P(), P(), P(), P("dp", ctx, None)),
        out_specs=(P("dp", ctx, None), P(ctx, None), P(ctx, None), P()),
        check_vma=False,
    )
```

```python
import functools
import math

import jax
import jax.numpy as jnp
from jax import lax
from jax.experimental import pallas as pl
from jax.experimental.pallas import tpu as pltpu
from jax.sharding import Mesh, PartitionSpec as P

epsilon = 1e-06
D = 384
VIEWS = 8
HEAD = D // VIEWS
T = 128
W = 256
X_CHIPS, Z_CHIPS, CORES = 4, 8, 2
SHARES = X_CHIPS * Z_CHIPS
ROWS = D // (SHARES * CORES)
HALF = 7 * T
SQUARE = 4
AWAY = (3, 2, 1)
QUARTER = HALF // SQUARE
PICK = 16
BLOCKS = [("a", 0, 1), ("a", 0, 2), ("a", 1, 2), ("pair", 0, 0), ("last", 0, 0)]
BLOCKS += [("b", i, j) for i in range(3) for j in range(3)]


def place_of(at):
    return at // 7, slice(at % 7 * T, (at % 7 + 1) * T)


def quarter_of(place):
    return pl.ds(pl.multiple_of(place * QUARTER, 8), QUARTER)


f32, bf16 = jnp.float32, jnp.bfloat16
NN = ((1,), (0,))
NT = ((1,), (1,))
TN = ((0,), (0,))


def split(a):
    high = a.astype(bf16)
    return high, (a - high.astype(f32)).astype(bf16)


def dot3(a, b, dims):
    (ca,), (cb,) = dims
    return lax.dot_general(
        jnp.concatenate([a[0], a[0], a[1]], axis=ca),
        jnp.concatenate([b[0], b[1], b[0]], axis=cb),
        (dims, ((), ())),
        preferred_element_type=f32,
    )


def row_dot3(a, b, dims):
    d = functools.partial(
        lax.dot_general, dimension_numbers=(dims, ((), ())), preferred_element_type=f32
    )
    both = d(jnp.concatenate(a, axis=0), b[0])
    return both[:PICK] + both[PICK:] + d(a[0], b[1])


def cut(pair, rows, cols):
    return pair[0][rows, cols], pair[1][rows, cols]


ALL = slice(None)
WINDOWS = (slice(0, W), slice(D - W, D))


def join(parts):
    one, two = parts
    return jnp.concatenate([one[:, :T], one[:, T:] + two[:, :T], two[:, T:]], axis=1)


def iotas():
    return (lax.broadcasted_iota(jnp.int32, (T, T), axis) for axis in range(2))


def gram_kernel(place_ref, x_hbm, u_hbm, *refs):
    keeps, sends, (x_ref, u_ref, pay_ref, sems) = refs[:SQUARE], refs[SQUARE : 2 * SQUARE], refs[2 * SQUARE :]
    step = x_ref.shape[0] // 2
    copies = []
    for part in range(2):
        piece = pl.ds(part * step, step)
        for at, (source, target) in enumerate(((x_hbm, x_ref), (u_hbm, u_ref))):
            copy = pltpu.make_async_copy(
                source.at[piece], target.at[piece], sems.at[part * 2 + at]
            )
            copy.start()
            copies.append(copy)
    d = functools.partial(
        lax.dot_general, dimension_numbers=(TN, ((), ())), preferred_element_type=f32
    )
    sums = []
    for part in range(2):
        piece = pl.ds(part * step, step)
        copies[2 * part].wait()
        copies[2 * part + 1].wait()
        xh, xl = split(x_ref[piece])
        uh, ul = split(u_ref[piece])
        wide = d(xh, jnp.concatenate([xh, xl, uh, ul], axis=1))
        mixed = wide[:, 2 * D : 3 * D] + wide[:, 3 * D :] + d(xl, uh)
        sums.append((wide[:, :D], wide[:, D : 2 * D], mixed))
    whole, cross, mixed = (one + two for one, two in zip(*sums))
    a = whole + cross + cross.T
    for at, (name, i, j) in enumerate(BLOCKS):
        if name in ("a", "b"):
            source = a if name == "a" else mixed
            pay_ref[place_of(at)] = source[i * T : (i + 1) * T, j * T : (j + 1) * T]
    row, col = iotas()
    first, second, third = (a[i * T : (i + 1) * T, i * T : (i + 1) * T] for i in range(3))
    diagonal = jnp.sum(jnp.where(row == col, second, 0.0), axis=0, keepdims=True)
    hidden = jnp.where(row == T - 1, diagonal, diagonal[:, T - 1 :])
    pay_ref[place_of(3)] = jnp.where(row <= col, first, second)
    pay_ref[place_of(4)] = jnp.where(row <= col, third, hidden)
    core, chip = place_ref[0], place_ref[2]
    for k in range(SQUARE):
        to = chip ^ k
        keeps[k][...] = pay_ref[core, quarter_of(to)]
        sends[k][...] = pay_ref[1 - core, quarter_of(to)]


def heads_of(shape, axis, window):
    feature = lax.broadcasted_iota(jnp.int32, shape, axis) + window * (D - W)
    head = jnp.zeros(shape, jnp.int32)
    for h in range(1, VIEWS):
        head = head + jnp.where(feature >= h * HEAD, 1, 0)
    return feature, head


def masks(window):
    _, rows = heads_of((W, W), 0, window)
    _, cols = heads_of((W, W), 1, window)
    own = (rows < VIEWS // 2) if window == 0 else (rows >= VIEWS // 2)
    return (rows == cols) & own


def eye_of(size):
    return lax.broadcasted_iota(jnp.int32, (size, size), 0) == lax.broadcasted_iota(
        jnp.int32, (size, size), 1
    )


def to_col(eye, v):
    return jnp.sum(jnp.where(eye, v, 0.0), axis=1, keepdims=True)


def to_row(eye, v):
    return jnp.sum(jnp.where(eye, v, 0.0), axis=0, keepdims=True)


def sharp_col(sharp_ref, window):
    _, head = heads_of((W, 1), 0, window)
    sharp = jnp.zeros((W, 1), f32)
    for h in range(VIEWS):
        sharp = jnp.where(head == h, sharp_ref[h], sharp)
    return sharp


def rows_of(first, load, size):
    base = jnp.minimum(first // 8 * 8, size - PICK)
    block = load(pl.ds(pl.multiple_of(base, 8), PICK))
    return pltpu.roll(block, PICK - (first - base), 0)


scale = 1.0 / math.sqrt(262144)


def solve_kernel(
    place_ref, sharp_ref, w_ref, f_ref, m0, m1, m2, m3, o0, o1, o2, o3,
    gv_ref, m_ref, d_ref, rows_ref, block_ref, a_ref, b_ref, c_ref, t_ref, att_ref,
):
    core, first, chip = place_ref[0], place_ref[1], place_ref[2]
    for k, mine_ref, other_ref in zip((0,) + AWAY, (m0, m1, m2, m3), (o0, o1, o2, o3)):
        block_ref[core, quarter_of(chip ^ k)] = mine_ref[...]
        block_ref[1 - core, quarter_of(chip ^ k)] = other_ref[...]
    for at, (name, i, j) in enumerate(BLOCKS):
        if name in ("a", "b"):
            block = block_ref[place_of(at)]
            ref = a_ref if name == "a" else b_ref
            ref[i * T : (i + 1) * T, j * T : (j + 1) * T] = block
            if name == "a":
                ref[j * T : (j + 1) * T, i * T : (i + 1) * T] = block.T
    row, col = iotas()
    pair, last = block_ref[place_of(3)], block_ref[place_of(4)]
    pair_t = pair.T
    diagonal = jnp.where(col[:1] == T - 1, last[T // 2 : T // 2 + 1, :1], last[T - 1 :])
    a_ref[:T, :T] = jnp.where(row <= col, pair, pair_t)
    second = jnp.where(row > col, pair, pair_t)
    a_ref[T : 2 * T, T : 2 * T] = jnp.where(row == col, diagonal, second)
    a_ref[2 * T :, 2 * T :] = jnp.where(row <= col, last, last.T)
    a_s, b_s = split(a_ref[...]), split(b_ref[...])
    ws, fs = split(w_ref[...]), split(f_ref[...])
    tk = dot3(a_s, cut(ws, ALL, slice(D, 2 * D)), NN)
    c = dot3(cut(ws, ALL, slice(2 * D, 3 * D)), b_s, TN)
    tks, c_s = split(tk), split(c)
    raw = [dot3(cut(ws, ALL, span), cut(tks, ALL, span), TN) for span in WINDOWS]
    tq = dot3(a_s, cut(ws, ALL, slice(0, D)), NN)
    t_ref[:, :D], t_ref[:, D:] = tq, tk
    c_ref[...] = c
    attention_grads = [
        dot3(cut(fs, span, ALL), cut(c_s, span, ALL), NT) for span in WINDOWS
    ]
    q_square = jnp.sum(w_ref[:, :D] * tq, axis=0, keepdims=True)
    k_square = jnp.sum(w_ref[:, D : 2 * D] * tk, axis=0, keepdims=True)
    q_inv = lax.rsqrt(jnp.maximum(q_square, 0.0) + epsilon)
    k_inv = lax.rsqrt(jnp.maximum(k_square, 0.0) + epsilon)
    t_rows = rows_of(first, lambda rows: t_ref[rows], D)
    b_rows = rows_of(first, lambda rows: b_ref[rows], D)
    tq_rows, tk_rows = split(t_rows[:, :D]), split(t_rows[:, D:])
    eye = eye_of(W)
    attentions, covs, mixers = [], [], []
    for window, span in enumerate(WINDOWS):
        same = masks(window)
        cov = raw[window] * to_col(eye, q_inv[:, span]) * k_inv[:, span]
        cov = jnp.where(same, jnp.clip(cov, -1.0, 1.0), 0.0)
        table = jnp.where(same, jnp.exp(sharp_col(sharp_ref, window) * cov), 0.0)
        total = jnp.sum(table, axis=1, keepdims=True)
        attention = table / jnp.where(total > 0.0, total, 1.0)
        att_ref[window] = attention
        attentions.append(attention)
        covs.append(cov)
        mixers.append(dot3(cut(fs, span, ALL), split(attention), TN))
    gv = split(join(mixers))
    gv_ref[0], gv_ref[1] = gv
    window = jnp.where(first >= D // 2, 1, 0)
    offset = pl.multiple_of(window * (D - W), T)
    att_rows = rows_of(first - offset, lambda rows: att_ref[window, rows], W)
    c_part = split(c_ref[pl.ds(offset, W)])
    rows_ref[:, 2 * D : 3 * D] = row_dot3(split(b_rows), gv, NN)[:8] * scale
    rows_ref[:, 3 * D : 4 * D] = row_dot3(split(att_rows), c_part, NN)[:8] * scale
    q_sum, k_sum, q_rows, k_rows = [], [], [], []
    temp = jnp.zeros((1, T), f32)
    for window, span in enumerate(WINDOWS):
        attention, cov = attentions[window], covs[window]
        sharp = sharp_col(sharp_ref, window)
        attention_grad = attention_grads[window]
        inner = jnp.sum(attention * attention_grad, axis=1, keepdims=True)
        score_grad = attention * (attention_grad - inner)
        weighed = score_grad * cov
        by_feature = jnp.sum(weighed, axis=1, keepdims=True)
        q_sum.append(to_row(eye, sharp * by_feature))
        k_sum.append(jnp.sum(sharp * weighed, axis=0, keepdims=True))
        m_s = split(sharp * score_grad * to_col(eye, q_inv[:, span]) * k_inv[:, span])
        m_ref[0, window], m_ref[1, window] = m_s
        q_rows.append(row_dot3(cut(tk_rows, ALL, span), m_s, NT))
        k_rows.append(row_dot3(cut(tq_rows, ALL, span), m_s, NN))
        _, head = heads_of((W, T), 0, window)
        lane = lax.broadcasted_iota(jnp.int32, (W, T), 1)
        temp += jnp.sum(jnp.where(head == lane, by_feature, 0.0), axis=0, keepdims=True)
    d_q = join(q_sum) * (q_inv * q_inv)
    d_k = join(k_sum) * (k_inv * k_inv)
    d_ref[0:1] = d_q
    d_ref[1:2] = d_k
    rows_ref[:, :D] = (join(q_rows) - t_rows[:, :D] * d_q)[:8] * scale
    rows_ref[:, D : 2 * D] = (join(k_rows) - t_rows[:, D:] * d_k)[:8] * scale
    rows_ref[:, 4 * D :] = jnp.broadcast_to(temp * scale, (8, T))


def output_kernel(
    x_ref, u_ref, w_ref, gv_ref, m_ref, d_ref, out_hbm, out_ref, sems
):
    ws = split(w_ref[...])
    q_parts, k_parts = [], []
    for window, span in enumerate(WINDOWS):
        m_s = (m_ref[0, window], m_ref[1, window])
        q_parts.append(dot3(cut(ws, ALL, slice(D + span.start, D + span.stop)), m_s, NT))
        k_parts.append(dot3(cut(ws, ALL, span), m_s, NN))
    gq = split(join(q_parts) - w_ref[:, :D] * d_ref[0:1])
    gk = split(join(k_parts) - w_ref[:, D : 2 * D] * d_ref[1:2])
    g = tuple(jnp.concatenate([one, two], axis=1) for one, two in zip(gq, gk))
    gv = (gv_ref[0], gv_ref[1])
    wqk = cut(ws, ALL, slice(0, 2 * D))
    corner = dot3(cut(g, slice(0, T), ALL), cut(wqk, slice(0, T), ALL), NT)
    others = dot3(g, cut(wqk, slice(T, D), ALL), NT)
    corner = jnp.concatenate([corner, others[:T, :T].T, others[:T, T:].T], axis=0)
    p = split(jnp.concatenate([corner, others], axis=1))
    r = split(dot3(gv, cut(ws, ALL, slice(2 * D, 3 * D)), NT))
    factors = tuple(jnp.concatenate([one, two], axis=0) for one, two in zip(p, r))
    tokens = x_ref.shape[0]
    step = tokens // 8
    copies = []
    for k in range(8):
        piece = pl.ds(k * step, step)
        xs, us = split(x_ref[piece]), split(u_ref[piece])
        token = tuple(jnp.concatenate([one, two], axis=1) for one, two in zip(xs, us))
        out_ref[piece] = dot3(token, factors, NN)
        copy = pltpu.make_async_copy(out_ref.at[piece], out_hbm.at[piece], sems.at[k])
        copy.start()
        copies.append(copy)
    for copy in copies:
        copy.wait()


def total_kernel(own_ref, two_ref, three_ref, one_ref, mixer_ref, output_ref, sharp_ref):
    total = (own_ref[...] + two_ref[...]) + (one_ref[...] + three_ref[...])
    mixer_ref[...] = total[:ROWS, : 3 * D]
    output_ref[...] = total[:ROWS, 3 * D : 4 * D]
    sharp_ref[...] = total[0:1, 4 * D : 4 * D + VIEWS]


smem = pl.BlockSpec(memory_space=pltpu.SMEM)
vmem = pl.BlockSpec(memory_space=pltpu.VMEM)
hbm = pl.BlockSpec(memory_space=pltpu.HBM)


def call(kernel, ins, outs, shapes, scratch=(), flops=0, limit=32):
    return pl.pallas_call(
        kernel,
        in_specs=ins,
        out_specs=outs,
        out_shape=[jax.ShapeDtypeStruct(*one) for one in shapes],
        scratch_shapes=list(scratch),
        compiler_params=pltpu.CompilerParams(vmem_limit_bytes=limit * 1024 * 1024),
        cost_estimate=pl.CostEstimate(flops=flops, bytes_accessed=4 * 1024 * 1024, transcendentals=0),
    )


def body(
    incoming_embeddings,
    stacked_projector,
    final_projector,
    sharpness_per_view,
    upstream_sensitivity,
):
    x = incoming_embeddings[0]
    u = upstream_sensitivity[0]
    tokens = x.shape[0]
    core, x_chip, z_chip = (lax.axis_index(axis) for axis in ("core", "x", "z"))
    ctx = (x_chip * Z_CHIPS + z_chip) * CORES + core
    chip = (x_chip ^ x_chip // 2) % 2 * 2 + z_chip % 2
    place = jnp.stack([core, ctx * ROWS, chip]).astype(jnp.int32)
    unit = 2 * 3 * D * D * D

    def in_hbm(array):
        return pltpu.with_memory_space_constraint(array, pltpu.HBM)

    quarter = ((QUARTER, T), f32)
    pieces = call(
        gram_kernel,
        [smem, hbm, hbm],
        [vmem] * 2 * SQUARE,
        [quarter] * 2 * SQUARE,
        [
            pltpu.VMEM((tokens, D), f32),
            pltpu.VMEM((tokens, D), f32),
            pltpu.VMEM((CORES, HALF, T), f32),
            pltpu.SemaphoreType.DMA((4,)),
        ],
        flops=6 * unit,
    )(place, in_hbm(x), in_hbm(u))

    def swap(array):
        return lax.ppermute(array, "core", [(0, 1), (1, 0)])

    def shift(array, axis, by):
        size = lax.axis_size(axis)
        return lax.ppermute(array, axis, [(i, (i + by) % size) for i in range(size)])

    def exchange(array, x_apart, z_apart):
        pairs = [
            (i * Z_CHIPS + j, (i ^ x_apart) * Z_CHIPS + (j ^ z_apart))
            for i in range(X_CHIPS)
            for j in range(Z_CHIPS)
        ]
        return lax.ppermute(array, ("x", "z"), pairs)

    def within_square(pieces):
        return [exchange(piece, k // 2, k % 2) for k, piece in zip(AWAY, pieces)]

    part = [keep + swap(send) for keep, send in zip(pieces[:SQUARE], pieces[SQUARE:])]
    others = [exchange(part[k], k // 2, k % 2) for k in reversed(AWAY)]
    part = (part[0] + others[0]) + (others[1] + others[2])
    for apart in ((3, 0), (0, 6), (0, 2)):
        part = part + exchange(part, *apart)
    mine = [part] + within_square([part] * 3)
    other = [swap(piece) for piece in mine]

    gv, m, diagonal, rows = call(
        solve_kernel,
        [smem, smem] + [vmem] * 10,
        [vmem] * 4,
        [((2, D, D), bf16), ((2, 2, W, W), bf16), ((2, D), f32), ((8, 4 * D + T), f32)],
        [
            pltpu.VMEM((CORES, HALF, T), f32),
            pltpu.VMEM((D, D), f32),
            pltpu.VMEM((D, D), f32),
            pltpu.VMEM((D, D), f32),
            pltpu.VMEM((D, 2 * D), f32),
            pltpu.VMEM((2, W, W), f32),
        ],
        flops=8 * unit,
    )(place, sharpness_per_view, stacked_projector, final_projector, *mine, *other)

    one, two, three = [shift(rows, "dp", k) for k in range(1, lax.axis_size("dp"))]
    (input_grad,) = call(
        output_kernel,
        [vmem] * 6,
        [hbm],
        [((tokens, D), f32)],
        [pltpu.VMEM((tokens, D), f32), pltpu.SemaphoreType.DMA((8,))],
        flops=12 * unit,
    )(x, u, stacked_projector, gv, m, diagonal)
    mixer_grad, output_grad, sharpness_grad = call(
        total_kernel,
        [vmem] * 4,
        [vmem] * 3,
        [((ROWS, 3 * D), f32), ((ROWS, D), f32), ((1, VIEWS), f32)],
    )(rows, two, three, one)
    return input_grad[None], mixer_grad, output_grad, sharpness_grad.reshape(VIEWS)


def solution(mesh):
    slides = mesh.shape["dp"]
    fine = Mesh(
        mesh.devices.reshape(slides, X_CHIPS, Z_CHIPS, CORES), ("dp", "x", "z", "core")
    )
    ctx = ("x", "z", "core")
    return jax.shard_map(
        body,
        mesh=fine,
        in_specs=(P("dp", ctx, None), P(), P(), P(), P("dp", ctx, None)),
        out_specs=(P("dp", ctx, None), P(ctx, None), P(ctx, None), P()),
        check_vma=False,
    )
```
